512 devices in a mesh: lat: 16 (over x, y_lo, core), lon: 32 (over y_hi, z).
Axes of the slice: x: 4, y: 8 (y_hi: 4, y_lo: 2; y = y_hi * 2 + y_lo), z: 8, core: 2. Of those that a mesh axis runs over, the one named last changes fastest.
Arguments:
- fields: bfloat16 [256, 512, 384], P('lat', 'lon'), may hold values from -6 to 6
- spectral_gain: float32 [192, 384], P(None, 'lon'), may hold values from -4 to 4
- stencil_one: bfloat16 [256, 3, 5, 13], P('lat'), may hold values from -1 to 1
- stencil_two: bfloat16 [256, 3, 5, 13], P('lat'), may hold values from -1 to 1
- cycle_reach: int32 [256], P('lat'), may hold values from 1 to 6, as said below
- mix_one: bfloat16 [3, 384, 384], replicated, may hold values from -0.1875 to 0.1875
- mix_two: bfloat16 [3, 384, 384], replicated, may hold values from -0.1875 to 0.1875
- norm_gain: float32 [384], replicated, may hold values from 0.1 to 1.9
- w_in: bfloat16 [384, 768], replicated, may hold values from -0.3125 to 0.3125
- w_out: bfloat16 [768, 384], replicated, may hold values from -0.21875 to 0.21875
Outputs:
- block_out: bfloat16 [256, 512, 384], P('lat', 'lon')
The draws below stay inside these ranges and needn't reach their ends.
Inputs may be any that keep to these rules, and one draw needn't show every extreme that they name: `cycle_reach`: the cycles nearest the two poles reach 6 cells.
All inputs are finite; a program needn't handle non-finite values.
Results may differ from the reference program's by a relative error of at most 0.013.
Values may be sent and summed in bfloat16 or wider, within the bound.
No kernel may reach another device: no remote copies, remote signals or barrier semaphores. Data moves between devices by JAX's collectives and lax.ppermute only.
A program may use at most 64 MiB of HBM per device.

```python
import math
import jax
import jax.numpy as jnp
from jax import lax

C = 384
HID = 768
NBASIS = 3
RLAT = 2
RLON = 6
LAT_DEV = 16
LON_DEV = 16
LMAX = 192
NLAT = 256
NLON = 512
N_LAT = 16
N_LON = 32


def draw_cycle_reach(key, part):
    key = jax.random.fold_in(key, 7)
    position = jnp.arange(NLAT, dtype=jnp.int32)
    distance = jnp.abs(2 * position - (NLAT - 1))
    base_reach = 1 + (RLON - 1) * distance // (NLAT - 1)
    jitter = jax.random.randint(key, (NLAT,), 0, 2, dtype=jnp.int32)
    return jnp.minimum(base_reach + jitter, RLON).astype(jnp.int32)


def shard_levels(own_key, dims, split, least, top_value):
    def one(axis_at, shards_of):
        draws = jax.random.uniform(jax.random.fold_in(jax.random.fold_in(own_key, 6), axis_at), (shards_of,), jnp.float32, least / len(split), top_value / len(split))
        return jnp.repeat(jnp.exp(draws), dims[axis_at] // shards_of).reshape((-1,) + (1,) * (len(dims) - axis_at - 1))

    level = one(*split[0])
    for cut in split[1:]:
        level = level * one(*cut)
    return level


def noise(own_key, shape, scale, most, cuts=(), kind=jnp.bfloat16):
    drawn = scale * jax.random.normal(own_key, shape, jnp.float32)
    if cuts:
        drawn = drawn * shard_levels(own_key, shape, cuts, -0.22, 0.18)
    return jnp.clip(drawn, -most, most).astype(kind)


def setup_inputs(seed: int = 0) -> dict:
    key_list = jax.random.split(jax.random.key(seed), 11)
    fields = noise(key_list[0], (NLAT, NLON, C), 1.0, 6.0, ((0, 16), (1, 32)))
    spectral_gain = noise(key_list[1], (LMAX, C), 1.0, 4.0, ((1, 32),), jnp.float32)
    stencil_one = noise(key_list[2], (NLAT, NBASIS, 2 * RLAT + 1, 2 * RLON + 1), 0.18, 1.0, ((0, 16),))
    stencil_two = noise(key_list[3], (NLAT, NBASIS, 2 * RLAT + 1, 2 * RLON + 1), 0.18, 1.0, ((0, 16),))
    cycle_reach = draw_cycle_reach(jax.random.fold_in(key_list[10], 71), 0)
    mix_one = noise(key_list[5], (NBASIS, C, C), (NBASIS * C) ** -0.5, 0.1875)
    mix_two = noise(key_list[6], (NBASIS, C, C), (NBASIS * C) ** -0.5, 0.1875)
    norm_gain = jnp.clip(1.0 + 0.18 * jax.random.normal(key_list[7], (C,), jnp.float32), 0.1, 1.9)
    w_in = noise(key_list[8], (C, HID), C ** -0.5, 0.3125)
    w_out = noise(key_list[9], (HID, C), HID ** -0.5, 0.21875)
    return {"fields": fields, "spectral_gain": spectral_gain, "stencil_one": stencil_one, "stencil_two": stencil_two, "cycle_reach": cycle_reach, "mix_one": mix_one, "mix_two": mix_two, "norm_gain": norm_gain, "w_in": w_in, "w_out": w_out}


def legendre_table(colatitude, orders, degrees):
    order_vals = orders.astype(jnp.float32)
    counter = jnp.arange(1, degrees + 1, dtype=jnp.int32).astype(jnp.float32)
    factors = jnp.log((2.0 * counter - 1.0) / (2.0 * counter))
    partial_sum = lax.optimization_barrier(jnp.sum(jnp.where(counter[None, :] <= order_vals[:, None], factors[None, :], 0.0), axis=1))
    log_sine = jnp.log(jnp.sin(colatitude))
    start_log = 0.5 * jnp.log((2.0 * order_vals + 1.0) / (4.0 * math.pi)) + 0.5 * partial_sum
    diagonal = jnp.exp(start_log[None, :] + order_vals[None, :] * log_sine[:, None])
    cosine = jnp.cos(colatitude)[:, None]
    squared_m = order_vals * order_vals

    def advance(state_pair, degree):
        previous, earlier = state_pair
        degree_f = degree.astype(jnp.float32)
        coef_up = jnp.sqrt(jnp.maximum(4.0 * degree_f * degree_f - 1.0, 0.0) / jnp.maximum(degree_f * degree_f - squared_m, 1.0))
        degree_b = degree_f - 1.0
        coef_down = jnp.sqrt(jnp.maximum(degree_b * degree_b - squared_m, 0.0) / jnp.maximum(4.0 * degree_b * degree_b - 1.0, 1.0))
        entry = coef_up[None, :] * (cosine * previous - coef_down[None, :] * earlier)
        entry = jnp.where(degree == orders[None, :], diagonal, entry)
        entry = jnp.where(degree < orders[None, :], jnp.zeros_like(entry), entry)
        return ((entry, previous), entry)
    zero_field = jnp.zeros((colatitude.shape[0], orders.shape[0]), jnp.float32)
    _, stacked = lax.scan(advance, (zero_field, zero_field), jnp.arange(degrees, dtype=jnp.int32))
    return stacked

def fourier_angles(orders, lon_count):
    cells = jnp.arange(lon_count, dtype=jnp.int32)
    product = orders[:, None] * cells[None, :] % lon_count
    return 2.0 * math.pi / lon_count * product.astype(jnp.float32)

def disco_reference(field, stencil, mixing, cycle_reach):
    tap_count = 2 * RLON + 1
    offsets = jnp.arange(tap_count, dtype=jnp.int32) - RLON
    inside = (jnp.abs(offsets)[None, :] <= cycle_reach[:, None]).astype(jnp.bfloat16)
    masked = (stencil * inside[:, None, None, :]).astype(jnp.float32)
    padded = jnp.pad(field.astype(jnp.float32), ((RLAT, RLAT), (0, 0), (0, 0)))
    wrapped = jnp.concatenate([padded[:, NLON - RLON:], padded, padded[:, :RLON]], axis=1)
    width_ext = LON_DEV + 2 * RLON
    window = jnp.arange(N_LON, dtype=jnp.int32)[:, None] * LON_DEV + jnp.arange(width_ext, dtype=jnp.int32)[None, :]
    tap_ids = jnp.arange(tap_count, dtype=jnp.int32)
    out_ids = jnp.arange(LON_DEV, dtype=jnp.int32)
    in_ids = jnp.arange(width_ext, dtype=jnp.int32)
    one_hot = (in_ids[None, None, :] - out_ids[None, :, None] == tap_ids[:, None, None]).astype(jnp.float32)
    mixing_f = mixing.astype(jnp.float32)

    def one_slab(number):
        first_row = number * LAT_DEV
        slab_rows = lax.dynamic_slice_in_dim(wrapped, first_row, LAT_DEV + 2 * RLAT, 0)
        sectors = slab_rows[:, window]
        stacked = jnp.stack([sectors[row_shift:row_shift + LAT_DEV] for row_shift in range(2 * RLAT + 1)], axis=1)
        weights = lax.dynamic_slice_in_dim(masked, first_row, LAT_DEV, 0)
        banded = jnp.einsum('akdt,tjn->akdjn', weights, one_hot, precision=lax.Precision.HIGHEST)
        gathered = jnp.einsum('akdjn,adsnc->aksjc', banded, stacked, precision=lax.Precision.HIGHEST)
        gathered = gathered.reshape(LAT_DEV, NBASIS, NLON, C).astype(jnp.bfloat16)
        gathered = lax.optimization_barrier(gathered).astype(jnp.float32)
        return jnp.einsum('akjc,kce->aje', gathered, mixing_f, precision=lax.Precision.HIGHEST)
    result = lax.map(one_slab, jnp.arange(N_LAT, dtype=jnp.int32))
    return result.reshape(NLAT, NLON, C)

def finish(stream, second, norm_gain, w_in, w_out):
    summed = stream.astype(jnp.float32) + second
    center = summed - lax.optimization_barrier(jnp.mean(summed, axis=-1, keepdims=True))
    spread = lax.optimization_barrier(jnp.mean(center * center, axis=-1, keepdims=True))
    normed = (center * lax.rsqrt(spread + 1e-05) * norm_gain).astype(jnp.bfloat16)
    shape_out = normed.shape
    flat = normed.reshape(-1, shape_out[-1])
    hidden = jax.nn.gelu(jnp.dot(flat, w_in, preferred_element_type=jnp.float32)).astype(jnp.bfloat16)
    update = jnp.dot(hidden, w_out, preferred_element_type=jnp.float32).reshape(shape_out)
    return (stream.astype(jnp.float32) + update).astype(jnp.bfloat16)

def reference(fields, spectral_gain, stencil_one, stencil_two, cycle_reach, mix_one, mix_two, norm_gain, w_in, w_out):
    orders = jnp.arange(LMAX, dtype=jnp.int32)
    colatitude = math.pi * (jnp.arange(NLAT, dtype=jnp.int32).astype(jnp.float32) + 0.5) / NLAT
    quad_weight = math.pi / NLAT * (2.0 * math.pi / NLON) * jnp.sin(colatitude)
    angles = fourier_angles(orders, NLON)
    forward_table = jnp.stack([jnp.cos(angles).T, -jnp.sin(angles).T], axis=1).astype(jnp.bfloat16).astype(jnp.float32)
    doubling = jnp.where(orders == 0, 1.0, 2.0).astype(jnp.float32)[:, None]
    inverse_table = jnp.stack([doubling * jnp.cos(angles), -doubling * jnp.sin(angles)], axis=0)
    spectra = jnp.einsum('inc,nrm->irmc', fields.astype(jnp.float32), forward_table, precision=lax.Precision.HIGHEST)
    weighted = spectra * quad_weight[:, None, None, None]
    order_share = LMAX // N_LAT

    def one_group(number):
        picked = lax.dynamic_slice_in_dim(orders, number * order_share, order_share, 0)
        plm_table = legendre_table(colatitude, picked, LMAX)
        portion = lax.dynamic_slice_in_dim(weighted, number * order_share, order_share, 2)
        harmonics = jnp.einsum('irmc,lim->lrmc', portion, plm_table, precision=lax.Precision.HIGHEST)
        harmonics = harmonics * spectral_gain[:, None, None, :]
        return jnp.einsum('lrmc,lim->irmc', harmonics, plm_table, precision=lax.Precision.HIGHEST)
    groups = lax.map(one_group, jnp.arange(N_LAT, dtype=jnp.int32))
    returned = jnp.transpose(groups, (1, 2, 0, 3, 4)).reshape(NLAT, 2, LMAX, C)
    spectral = jnp.einsum('irmc,rmn->inc', returned, inverse_table, precision=lax.Precision.HIGHEST).astype(jnp.bfloat16)
    first = disco_reference(fields, stencil_one, mix_one, cycle_reach)
    stream = (fields.astype(jnp.float32) + spectral.astype(jnp.float32) + first).astype(jnp.bfloat16)
    second = disco_reference(stream, stencil_two, mix_two, cycle_reach)
    return finish(stream, second, norm_gain, w_in, w_out)
```

```python
import functools
import math

import jax
import jax.numpy as jnp
from jax import lax
from jax.experimental import pallas as pl
from jax.experimental.pallas import tpu as pltpu
from jax.sharding import PartitionSpec as P

C = 384
CL = 12
CP = 16
KB = 3
RLAT = 2
RLON = 6
TAPS = 2 * RLON + 1
DLAT = 2 * RLAT + 1
NLAT = 256
NLON = 512
PLAT = 16
PLON = 32
A = 16
N = 16
M = 192
ML = 12
AX = A + 2 * RLAT
JX = 32
OFF = 8
F32 = jnp.float32
BF = jnp.bfloat16
NT = (((1,), (1,)), ((), ()))
VMEM_LIMIT = 48 * 1024 * 1024


def call(kernel, outs, scratch, *args, smem=(), flops=1_000_000, moved=1_000_000):
    specs = [
        pl.BlockSpec(memory_space=pltpu.SMEM if i in smem else pltpu.VMEM)
        for i in range(len(args))
    ]
    out_specs = jax.tree.map(lambda _: pl.BlockSpec(memory_space=pltpu.VMEM), outs)
    return pl.pallas_call(
        kernel,
        out_shape=outs,
        in_specs=specs,
        out_specs=out_specs,
        scratch_shapes=scratch,
        cost_estimate=pl.CostEstimate(flops=flops, bytes_accessed=moved, transcendentals=0),
        compiler_params=pltpu.CompilerParams(vmem_limit_bytes=VMEM_LIMIT),
    )(*args)


def swap_blocks(pieces, width):
    count = len(pieces)
    pieces = list(pieces)
    block = lax.broadcasted_iota(jnp.int32, pieces[0].shape, 1) // width
    step = 1
    while step < count:
        low = (block & step) == 0
        for i in range(count):
            if i & step:
                continue
            x, y = pieces[i], pieces[i | step]
            pieces[i] = jnp.where(low, x, pltpu.roll(y, step * width, 1))
            pieces[i | step] = jnp.where(low, pltpu.roll(x, 128 - step * width, 1), y)
        step *= 2
    return pieces


def prep_kernel(fields_ref, out_ref, rows):
    turned = fields_ref[...].reshape(A * N, C).astype(F32).T
    for hi in range(2):
        rows[pl.ds(hi, C, stride=2), :] = turned[:, hi * 128 : hi * 128 + 128]
    for d in range(PLON):
        out_ref[d] = rows[24 * d : 24 * d + 24, :].astype(BF)


def table_kernel(order_ref, cos_ref, diag_ref, out_ref, rows):
    order = order_ref[...]
    square = order * order
    cosine = [jnp.broadcast_to(cos_ref[:, h * 128 : h * 128 + 128], (CP, 128)) for h in range(2)]
    diag = [diag_ref[:, h * 128 : h * 128 + 128] for h in range(2)]
    zero = order * 0.0

    def step(degree, state):
        deg = jnp.full((CP, 128), degree, jnp.int32).astype(F32)
        back = deg - 1.0
        up = jnp.sqrt(jnp.maximum(4.0 * deg * deg - 1.0, 0.0) / jnp.maximum(deg * deg - square, 1.0))
        down = jnp.sqrt(
            jnp.maximum(back * back - square, 0.0) / jnp.maximum(4.0 * back * back - 1.0, 1.0)
        )
        new = []
        for h in range(2):
            previous, earlier = state[2 * h], state[2 * h + 1]
            entry = (up * cosine[h]) * previous - (up * down) * earlier
            entry = jnp.where(order == deg, diag[h], entry)
            rows[h, pl.ds(pl.multiple_of(degree * CP, CP), CP), :] = entry
            new += [entry, previous]
        return tuple(new)

    lax.fori_loop(0, M, step, (zero,) * 4, unroll=8)
    for m in range(ML):
        for h in range(2):
            out_ref[m, :, h * 128 : h * 128 + 128] = rows.at[h][
                pl.ds(m, M, stride=CP), :
            ].astype(BF)


def forward_kernel(recv_ref, u_ref, v_ref, c_ref, s_ref, out_ref, grid, rows):
    pieces = [
        jnp.concatenate([recv_ref[hi * 8 + lo].astype(F32) for hi in range(4)], axis=0)
        for lo in range(8)
    ]
    pieces = swap_blocks(pieces, 16)
    for hi in range(4):
        for lo in range(8):
            grid.at[hi][pl.ds(lo, 24, stride=8), :] = pieces[lo][hi * 24 : hi * 24 + 24]
        grid[hi, 192:256, :] = jnp.zeros((64, 128), F32)
    circles = jnp.concatenate([grid[hi].astype(BF) for hi in range(4)], axis=1)
    cosb, sinb = c_ref[...], s_ref[...]
    table = jnp.concatenate(
        [
            (u_ref[s : s + 1, :] * cosb + v_ref[s : s + 1, :] * sinb).astype(BF)
            for s in range(PLON)
        ],
        axis=0,
    )
    spectra = jnp.dot(circles, table, preferred_element_type=F32).T
    for g in range(2):
        rows[pl.ds(g, 2 * M, stride=2), :] = spectra[:, g * 128 : g * 128 + 128]
    for e in range(PLAT):
        out_ref[e] = rows[48 * e : 48 * e + 48, :].astype(BF)


def split(value):
    high = value.astype(BF)
    low = (value - high.astype(F32)).astype(BF)
    return jnp.concatenate([high, low], axis=0)


def legendre_kernel(recv_ref, tab_ref, quad_ref, gain_ref, out_ref, grid, res):
    pieces = [
        jnp.concatenate([recv_ref[hi * 8 + lo].astype(F32) for hi in range(2)], axis=0)
        for lo in range(8)
    ]
    pieces = swap_blocks(pieces, 16)
    for hi in range(2):
        for x in range(8):
            grid.at[hi][pl.ds(x, 48, stride=8), :] = pieces[x][hi * 48 : hi * 48 + 48]
    gain = gain_ref[...]
    quad = quad_ref[...]
    for m in range(ML):
        part = slice(32 * m, 32 * m + 32)
        weighted = jnp.concatenate([grid[0, part, :], grid[1, part, :]], axis=1) * quad
        table = tab_ref[m]
        both = lax.dot_general(split(weighted), table, NT, preferred_element_type=F32)
        harmonics = (both[:32] + both[32:]) * gain
        both = jnp.dot(split(harmonics), table, preferred_element_type=F32)
        result = both[:32] + both[32:]
        for r in range(2):
            at = (2 * m + r) * CL
            for h in range(2):
                res[h, at : at + CL, :] = result[16 * r : 16 * r + CL, h * 128 : h * 128 + 128]
    lanes = lax.broadcasted_iota(jnp.int32, (72, 128), 1)
    place = lanes // 32
    inner = lanes % 32
    source = [[res.at[h][pl.ds(lo, 72, stride=4), :] for lo in range(4)] for h in range(2)]
    for j in range(PLAT):
        total = None
        for lo in range(4):
            shift = (lo * 32 - (16 * j - RLAT)) % 128
            value = pltpu.roll(source[j // 8][lo], shift, 1) if shift else source[j // 8][lo]
            if j in (7, 8):
                other = source[1 - j // 8][lo]
                other = pltpu.roll(other, shift, 1) if shift else other
                bound = 128 - (16 * 7 - RLAT) if j == 7 else RLAT
                first, last = (value, other) if j == 7 else (other, value)
                value = jnp.where(inner < bound, first, last)
            total = value if total is None else jnp.where(place == lo, value, total)
        out_ref[j] = total.astype(BF)


def inverse_kernel(recv_ref, u_ref, v_ref, c_ref, s_ref, out_ref, rows, coef, grid):
    for e in range(PLAT):
        rows[72 * e : 72 * e + 72, :] = recv_ref[e].astype(F32)
    for hi in range(3):
        turned = rows[pl.ds(hi, 2 * M, stride=3), :].T
        for lo in range(4):
            at = (hi * 4 + lo) * AX
            coef[at : at + AX, :] = turned[lo * 32 : lo * 32 + AX, :]
    left = coef[...].astype(BF)
    cosb, sinb = c_ref[...], s_ref[...]
    for k in range(8):
        table = jnp.concatenate(
            [
                (u_ref[d : d + 1, :] * cosb + v_ref[d : d + 1, :] * sinb).astype(BF)
                for d in range(4 * k, 4 * k + 4)
            ],
            axis=0,
        )
        grid[k] = lax.dot_general(left, table, NT, preferred_element_type=F32)
    for k in range(8):
        pieces = [grid.at[k][pl.ds(lo, 60, stride=4), :] for lo in range(4)]
        pieces = swap_blocks(pieces, 32)
        for lo in range(4):
            out_ref[4 * k + lo] = pieces[lo].astype(BF)


def gather_rows(taps_ref, field, mixing_ref, gathered, rows, cols, wide, start):
    lanes = taps_ref.shape[1]
    for a in range(rows):
        bands = []
        for k in range(KB):
            line = taps_ref[a * KB + k : a * KB + k + 1, :]
            band = pltpu.roll(
                jnp.broadcast_to(line, (cols, lanes)), start, 1, stride=1, stride_axis=0
            )
            bands.append(band.astype(BF))
        band = jnp.concatenate(bands, axis=0)[:, : DLAT * wide]
        value = jnp.dot(
            band, field[a * wide : (a + DLAT) * wide, :], preferred_element_type=F32
        ).astype(BF)
        for k in range(KB):
            gathered[k, a * cols : (a + 1) * cols, :] = value[k * cols : (k + 1) * cols]
    total = jnp.dot(gathered[0], mixing_ref[0], preferred_element_type=F32)
    for k in range(1, KB):
        total += jnp.dot(gathered[k], mixing_ref[k], preferred_element_type=F32)
    return total


def first_kernel(rim_ref, left_ref, right_ref, taps_ref, mix_ref, out_ref, field, gathered):
    for a in range(AX + 2 * RLAT):
        field[48 * a : 48 * a + 16, :] = left_ref[a]
        field[48 * a + 16 : 48 * a + 32, :] = rim_ref[a]
        field[48 * a + 32 : 48 * a + 48, :] = right_ref[a]
    first = gather_rows(taps_ref, field, mix_ref, gathered, AX, JX, 48, 16 - OFF - RLON)
    for a in range(AX):
        at = (a + RLAT) * 48 + 16 - OFF
        own = field[(a + RLAT) * 48 : (a + RLAT) * 48 + 48, :].astype(F32)
        out_ref[a * JX : (a + 1) * JX, :] = (
            first[a * JX : (a + 1) * JX] + own[16 - OFF : 16 - OFF + JX]
        )


def last_kernel(
    place_ref, recv_ref, pre_ref, taps_ref, mix_ref, norm_ref, in_ref, back_ref, out_ref,
    rows, stream, exact, gathered,
):
    place = place_ref[0]
    for s in range(PLON):
        rows[60 * s : 60 * s + 60, :] = recv_ref[s].astype(F32)
    for hi in range(5):
        spectral = rows[pl.ds(hi, C, stride=5), :].T
        value = pre_ref[128 * hi : 128 * hi + 128, :] + spectral
        row = lax.broadcasted_iota(jnp.int32, (128, C), 0) // JX + 4 * hi - RLAT + place * A
        value = jnp.where((row >= 0) & (row < NLAT), value, 0.0).astype(BF)
        stream[128 * hi : 128 * hi + 128, :] = value
        exact[128 * hi : 128 * hi + 128, :] = value.astype(F32)
    second = gather_rows(taps_ref, stream, mix_ref, gathered, A, N, JX, OFF - RLON)
    own = jnp.concatenate(
        [exact[(a + RLAT) * JX + OFF : (a + RLAT) * JX + OFF + N, :] for a in range(A)], axis=0
    )
    summed = own + second
    center = summed - jnp.mean(summed, axis=-1, keepdims=True)
    spread = jnp.mean(center * center, axis=-1, keepdims=True)
    normed = (center * lax.rsqrt(spread + 1e-05) * norm_ref[...]).astype(BF)
    hidden = jax.nn.gelu(jnp.dot(normed, in_ref[...], preferred_element_type=F32)).astype(BF)
    update = jnp.dot(hidden, back_ref[...], preferred_element_type=F32)
    out_ref[...] = (own + update).astype(BF).reshape(A, N, C)


def circle(product):
    return 2.0 * math.pi / NLON * (product % NLON).astype(F32)


def sector_tables(cells, doubled):
    orders = jnp.arange(M, dtype=jnp.int32)
    sectors = N * jnp.arange(PLON, dtype=jnp.int32)
    outer = circle(sectors[:, None] * orders[None, :])
    inner = circle(cells[:, None] * orders[None, :])
    scale = jnp.where(orders == 0, 1.0, 2.0).astype(F32) if doubled else 1.0
    cos, sin = jnp.cos(outer) * scale, jnp.sin(outer) * scale
    u = jnp.stack([cos, -sin], axis=-1).reshape(PLON, 2 * M)
    v = jnp.stack([-sin, -cos], axis=-1).reshape(PLON, 2 * M)
    return u, v, jnp.repeat(jnp.cos(inner), 2, axis=1), jnp.repeat(jnp.sin(inner), 2, axis=1)


def legendre_start(colatitude, orders, degrees):
    order_vals = orders.astype(F32)
    counter = jnp.arange(1, degrees + 1, dtype=jnp.int32).astype(F32)
    factors = jnp.log((2.0 * counter - 1.0) / (2.0 * counter))
    partial_sum = jnp.sum(
        jnp.where(counter[None, :] <= order_vals[:, None], factors[None, :], 0.0), axis=1
    )
    log_sine = jnp.log(jnp.sin(colatitude))
    start_log = 0.5 * jnp.log((2.0 * order_vals + 1.0) / (4.0 * math.pi)) + 0.5 * partial_sum
    return jnp.exp(start_log[:, None] + order_vals[:, None] * log_sine[None, :])


def shifted(value, axis, by, closed):
    count = lax.axis_size(axis)
    pairs = [(i, (i + by) % count) for i in range(count) if closed or 0 <= i + by < count]
    return lax.ppermute(value, axis, pairs)


def tap_lines(stencil, cycle_reach, wide, lanes):
    rows = stencil.shape[0]
    offsets = jnp.arange(TAPS, dtype=jnp.int32) - RLON
    inside = (jnp.abs(offsets)[None, :] <= cycle_reach[:, None]).astype(BF)
    masked = stencil * inside[:, None, None, :]
    masked = jnp.pad(masked, ((0, 0), (0, 0), (0, 0), (0, wide - TAPS)))
    masked = masked.reshape(rows, KB, DLAT * wide)
    return jnp.pad(masked, ((0, 0), (0, 0), (0, lanes - DLAT * wide)))


def exchange(block, axis):
    return lax.all_to_all(block, axis, split_axis=0, concat_axis=0, tiled=True)


def shape(dims, dtype):
    return jax.ShapeDtypeStruct(dims, dtype)


def local(
    fields, spectral_gain, stencil_one, stencil_two, cycle_reach, mix_one, mix_two, norm_gain,
    w_in, w_out,
):
    place = lax.axis_index("lat")
    colatitude = math.pi * (jnp.arange(NLAT, dtype=jnp.int32).astype(F32) + 0.5) / NLAT
    quad = math.pi / NLAT * (2.0 * math.pi / NLON) * jnp.sin(colatitude)
    own_orders = place * ML + jnp.minimum(jnp.arange(CP, dtype=jnp.int32), ML - 1)
    diagonal = legendre_start(colatitude, own_orders, M)

    sent = call(
        prep_kernel, shape((PLON, 24, 128), BF), [pltpu.VMEM((768, 128), F32)], fields
    )
    recv = exchange(sent, "lon")

    lines_one = tap_lines(stencil_one, cycle_reach, 48, 256)
    lines_two = tap_lines(stencil_two, cycle_reach, JX, 256).reshape(A * KB, 256).astype(F32)
    edge = 2 * RLAT

    def packed(cells, lines):
        extra = jnp.pad(lines.reshape(1, 4, C), ((0, 0), (0, N - 4), (0, 0)))
        return jnp.concatenate([cells, extra], axis=0)

    above = shifted(packed(fields[A - edge :], lines_one[A - RLAT :]), "lat", 1, False)
    below = shifted(packed(fields[:edge], lines_one[:RLAT]), "lat", -1, False)
    rim = jnp.concatenate([above[:edge], fields, below[:edge]], axis=0)
    taps_one = (
        jnp.concatenate(
            [
                above[edge, :4].reshape(RLAT, KB, 256),
                lines_one,
                below[edge, :4].reshape(RLAT, KB, 256),
            ],
            axis=0,
        )
        .reshape(AX * KB, 256)
        .astype(F32)
    )
    left = shifted(rim, "lon", 1, True)
    right = shifted(rim, "lon", -1, True)

    table = call(
        table_kernel,
        shape((ML, M, NLAT), BF),
        [pltpu.VMEM((2, M * CP, 128), F32)],
        jnp.broadcast_to(own_orders.astype(F32)[:, None], (CP, 128)),
        jnp.cos(colatitude)[None, :],
        diagonal,
    )
    spectra = call(
        forward_kernel,
        shape((PLAT, 48, 128), BF),
        [pltpu.VMEM((4, 256, 128), F32), pltpu.VMEM((768, 128), F32)],
        recv,
        *sector_tables(jnp.arange(N, dtype=jnp.int32), False),
    )
    gathered = exchange(spectra, "lat")
    gain = jnp.pad(spectral_gain.T, ((0, CP - CL), (0, 0)))
    results = call(
        legendre_kernel,
        shape((PLAT, 72, 128), BF),
        [pltpu.VMEM((2, 384, 128), F32), pltpu.VMEM((2, 288, 128), F32)],
        gathered,
        table,
        quad[None, :],
        jnp.concatenate([gain, gain], axis=0),
    )
    returned = exchange(results, "lat")
    sectors = call(
        inverse_kernel,
        shape((PLON, 60, 128), BF),
        [
            pltpu.VMEM((1152, 128), F32),
            pltpu.VMEM((CL * AX, 2 * M), F32),
            pltpu.VMEM((8, CL * AX, 128), F32),
        ],
        returned,
        *sector_tables(jnp.arange(JX, dtype=jnp.int32) - OFF, True),
    )
    spectral = exchange(sectors, "lon")
    pre = call(
        first_kernel,
        shape((AX * JX, C), F32),
        [pltpu.VMEM(((AX + edge) * 48, C), BF), pltpu.VMEM((KB, AX * JX, C), BF)],
        rim,
        left,
        right,
        taps_one,
        mix_one,
    )
    return call(
        last_kernel,
        shape((A, N, C), BF),
        [
            pltpu.VMEM((1920, 128), F32),
            pltpu.VMEM((AX * JX, C), BF),
            pltpu.VMEM((AX * JX, C), F32),
            pltpu.VMEM((KB, A * N, C), BF),
        ],
        place.reshape(1),
        spectral,
        pre,
        lines_two,
        mix_two,
        norm_gain[None, :],
        w_in,
        w_out,
        smem=(0,),
    )


def solution(mesh):
    in_specs = (
        P("lat", "lon", None),
        P(None, "lon"),
        P("lat", None, None, None),
        P("lat", None, None, None),
        P("lat"),
        P(),
        P(),
        P(),
        P(),
        P(),
    )
    out_specs = P("lat", "lon", None)
    return jax.shard_map(local, mesh=mesh, in_specs=in_specs, out_specs=out_specs, check_vma=False)
```

```python
import functools
import math

import jax
import jax.numpy as jnp
from jax import lax
from jax.experimental import pallas as pl
from jax.experimental.pallas import tpu as pltpu
from jax.sharding import PartitionSpec as P

C = 384
CL = 12
CP = 16
KB = 3
RLAT = 2
RLON = 6
TAPS = 2 * RLON + 1
DLAT = 2 * RLAT + 1
NLAT = 256
NLON = 512
PLAT = 16
PLON = 32
A = 16
N = 16
M = 192
ML = 12
AX = A + 2 * RLAT
JX = 32
OFF = 8
LANES = 256
EDGE = 2 * RLAT
F32 = jnp.float32
BF = jnp.bfloat16
NT = (((1,), (1,)), ((), ()))
VMEM_LIMIT = 14 * 1024 * 1024
LAST_LIMIT = 61 * 1024 * 1024


def call(kernel, outs, scratch, *args, smem=(), hbm=(), limit=VMEM_LIMIT, moved=1.0):
    specs = [
        pl.BlockSpec(
            memory_space=pltpu.SMEM if i in smem else pltpu.HBM if i in hbm else pltpu.VMEM
        )
        for i in range(len(args))
    ]
    out_specs = jax.tree.map(lambda _: pl.BlockSpec(memory_space=pltpu.VMEM), outs)
    return pl.pallas_call(
        kernel,
        out_shape=outs,
        in_specs=specs,
        out_specs=out_specs,
        scratch_shapes=scratch,
        cost_estimate=pl.CostEstimate(
            flops=0, bytes_accessed=int(moved * 3_400_000), transcendentals=0
        ),
        compiler_params=pltpu.CompilerParams(vmem_limit_bytes=limit),
    )(*args)


def swap_blocks(pieces, width):
    count = len(pieces)
    pieces = list(pieces)
    block = lax.broadcasted_iota(jnp.int32, pieces[0].shape, 1) // width
    step = 1
    while step < count:
        low = (block & step) == 0
        for i in range(count):
            if i & step:
                continue
            x, y = pieces[i], pieces[i | step]
            pieces[i] = jnp.where(low, x, pltpu.roll(y, step * width, 1))
            pieces[i | step] = jnp.where(low, pltpu.roll(x, 128 - step * width, 1), y)
        step *= 2
    return pieces


def prep_kernel(fields_ref, out_ref, field, rows, sems):
    copies = [
        pltpu.make_async_copy(
            fields_ref.at[:, :, pl.ds(128 * g, 128)], field.at[g], sems.at[g]
        )
        for g in range(3)
    ]
    for copy in copies:
        copy.start()
    for g in range(3):
        copies[g].wait()
        turned = field[g].reshape(A * N, 128).astype(F32).T
        for hi in range(2):
            rows[pl.ds(256 * g + hi, 128, stride=2), :] = turned[:, hi * 128 : hi * 128 + 128]
    for d in range(PLON):
        out_ref[d] = rows[24 * d : 24 * d + 24, :].astype(BF)


def twiddle_kernel(place_ref, u_ref, v_ref, c_ref, s_ref, iu_ref, iv_ref, ic_ref, is_ref):
    lane = lax.broadcasted_iota(jnp.int32, (PLON, 2 * M), 1)
    row = lax.broadcasted_iota(jnp.int32, (PLON, 2 * M), 0)
    order = lane // 2

    def turn(product):
        return 2.0 * math.pi / NLON * (product & (NLON - 1)).astype(F32)

    outer = turn(row * N * order + (lane & 1) * (NLON // 4))
    cos, sin = jnp.cos(outer), -jnp.sin(outer)
    scale = jnp.where(order == 0, 1.0, 2.0)
    u_ref[...], v_ref[...] = cos, sin
    iu_ref[...], iv_ref[...] = cos * scale, sin * scale
    inner = turn((row - OFF) * order)
    cos, sin = jnp.cos(inner), jnp.sin(inner)
    ic_ref[...], is_ref[...] = cos, sin
    c_ref[...], s_ref[...] = cos[OFF : OFF + N], sin[OFF : OFF + N]


def place_taps(stencil_ref, reach_ref, out_ref, wide):
    offset = lax.broadcasted_iota(jnp.int32, (A, TAPS), 1) - RLON
    cycle = lax.broadcasted_iota(jnp.int32, (A, TAPS), 0)
    reach = jnp.zeros((A, TAPS), jnp.int32)
    for a in range(A):
        reach = jnp.where(cycle == a, reach_ref[a], reach)
    inside = jnp.abs(offset) <= reach
    for k in range(KB):
        total = None
        for d in range(DLAT):
            taps = jnp.where(inside, stencil_ref[k * DLAT + d].astype(F32), 0.0)
            taps = jnp.concatenate([taps, jnp.zeros((A, LANES - TAPS), F32)], axis=1)
            taps = pltpu.roll(taps, d * wide, 1) if d else taps
            total = taps if total is None else total + taps
        out_ref[k] = total


def table_kernel(
    order_ref, cos_ref, diag_ref, out_ref, rows
):
    order = order_ref[...]
    square = order * order
    cosine = [jnp.broadcast_to(cos_ref[:, h * 128 : h * 128 + 128], (CP, 128)) for h in range(2)]
    diag = [diag_ref[:, h * 128 : h * 128 + 128] for h in range(2)]
    zero = order * 0.0

    def step(degree, state):
        deg = jnp.full((CP, 128), degree, jnp.int32).astype(F32)
        back = deg - 1.0
        up = jnp.sqrt(jnp.maximum(4.0 * deg * deg - 1.0, 0.0) / jnp.maximum(deg * deg - square, 1.0))
        down = jnp.sqrt(
            jnp.maximum(back * back - square, 0.0) / jnp.maximum(4.0 * back * back - 1.0, 1.0)
        )
        new = []
        for h in range(2):
            previous, earlier = state[2 * h], state[2 * h + 1]
            entry = (up * cosine[h]) * previous - (up * down) * earlier
            entry = jnp.where(order == deg, diag[h], entry)
            rows[h, pl.ds(pl.multiple_of(degree * CP, CP), CP), :] = entry
            new += [entry, previous]
        return tuple(new)

    lax.fori_loop(0, M, step, (zero,) * 4, unroll=8)
    for m in range(ML):
        for h in range(2):
            out_ref[m, :, h * 128 : h * 128 + 128] = rows.at[h][
                pl.ds(m, M, stride=CP), :
            ].astype(BF)


def forward_kernel(recv_ref, u_ref, v_ref, c_ref, s_ref, out_ref, grid, rows):
    pieces = [
        jnp.concatenate([recv_ref[hi * 8 + lo].astype(F32) for hi in range(4)], axis=0)
        for lo in range(8)
    ]
    pieces = swap_blocks(pieces, 16)
    for hi in range(4):
        for lo in range(8):
            grid.at[hi][pl.ds(lo, 24, stride=8), :] = pieces[lo][hi * 24 : hi * 24 + 24]
        grid[hi, 192:256, :] = jnp.zeros((64, 128), F32)
    circles = jnp.concatenate([grid[hi].astype(BF) for hi in range(4)], axis=1)
    cosb, sinb = c_ref[...], s_ref[...]
    table = jnp.concatenate(
        [
            (u_ref[s : s + 1, :] * cosb + v_ref[s : s + 1, :] * sinb).astype(BF)
            for s in range(PLON)
        ],
        axis=0,
    )
    spectra = jnp.dot(circles, table, preferred_element_type=F32).T
    for g in range(2):
        rows[pl.ds(g, 2 * M, stride=2), :] = spectra[:, g * 128 : g * 128 + 128]
    for e in range(PLAT):
        out_ref[e] = rows[48 * e : 48 * e + 48, :].astype(BF)


def split(value):
    high = value.astype(BF)
    low = (value - high.astype(F32)).astype(BF)
    return jnp.concatenate([high, low], axis=0)


def legendre_kernel(recv_ref, tab_ref, quad_ref, gain_ref, out_ref, grid, res):
    pieces = [
        jnp.concatenate([recv_ref[hi * 8 + lo].astype(F32) for hi in range(2)], axis=0)
        for lo in range(8)
    ]
    pieces = swap_blocks(pieces, 16)
    for hi in range(2):
        for x in range(8):
            grid.at[hi][pl.ds(x, 48, stride=8), :] = pieces[x][hi * 48 : hi * 48 + 48]
    gain = gain_ref[...]
    quad = quad_ref[...]
    for m in range(ML):
        part = slice(32 * m, 32 * m + 32)
        weighted = jnp.concatenate([grid[0, part, :], grid[1, part, :]], axis=1) * quad
        table = tab_ref[m]
        both = lax.dot_general(split(weighted), table, NT, preferred_element_type=F32)
        harmonics = (both[:32] + both[32:]) * gain
        both = jnp.dot(split(harmonics), table, preferred_element_type=F32)
        result = both[:32] + both[32:]
        for r in range(2):
            at = (2 * m + r) * CL
            for h in range(2):
                res[h, at : at + CL, :] = result[16 * r : 16 * r + CL, h * 128 : h * 128 + 128]
    lanes = lax.broadcasted_iota(jnp.int32, (48, 128), 1)
    source = [[res.at[h][pl.ds(lo, 48, stride=6), :] for lo in range(6)] for h in range(2)]
    for j in range(PLAT):
        total = None
        for lo in range(6):
            shift = (lo * AX - (16 * j - RLAT)) % 128
            value = pltpu.roll(source[j // 8][lo], shift, 1) if shift else source[j // 8][lo]
            if j in (7, 8):
                other = source[1 - j // 8][lo]
                other = pltpu.roll(other, shift, 1) if shift else other
                bound = 128 - (16 * 7 - RLAT) if j == 7 else RLAT
                first, last = (value, other) if j == 7 else (other, value)
                value = jnp.where(lanes < lo * AX + bound, first, last)
            total = value if total is None else jnp.where(lanes >= lo * AX, value, total)
        out_ref[j] = total.astype(BF)


def inverse_kernel(recv_ref, u_ref, v_ref, c_ref, s_ref, out_ref, rows, coef, grid):
    for e in range(PLAT):
        rows[48 * e : 48 * e + 48, :] = recv_ref[e].astype(F32)
    for hi in range(2):
        turned = rows[pl.ds(hi, 2 * M, stride=2), :].T
        coef[hi * 6 * AX : (hi + 1) * 6 * AX, :] = turned[: 6 * AX, :]
    left = coef[...].astype(BF)
    cosb, sinb = c_ref[...], s_ref[...]
    for k in range(8):
        table = jnp.concatenate(
            [
                (u_ref[d : d + 1, :] * cosb + v_ref[d : d + 1, :] * sinb).astype(BF)
                for d in range(4 * k, 4 * k + 4)
            ],
            axis=0,
        )
        grid[k] = lax.dot_general(left, table, NT, preferred_element_type=F32)
    for k in range(8):
        pieces = [grid.at[k][pl.ds(lo, 60, stride=4), :] for lo in range(4)]
        pieces = swap_blocks(pieces, 32)
        for lo in range(4):
            out_ref[4 * k + lo] = pieces[lo].astype(BF)


def gather_rows(taps_ref, field, mixing_ref, gathered, rows, cols, wide, start):
    for a in range(rows):
        bands = []
        for k in range(KB):
            line = taps_ref[k, a : a + 1, :]
            band = pltpu.roll(
                jnp.broadcast_to(line, (cols, LANES)), start, 1, stride=1, stride_axis=0
            )
            bands.append(band.astype(BF))
        band = jnp.concatenate(bands, axis=0)[:, : DLAT * wide]
        value = jnp.dot(
            band, field[a * wide : (a + DLAT) * wide, :], preferred_element_type=F32
        ).astype(BF)
        for k in range(KB):
            gathered[k, a * cols : (a + 1) * cols, :] = value[k * cols : (k + 1) * cols]
    total = jnp.dot(gathered[0], mixing_ref[0], preferred_element_type=F32)
    for k in range(1, KB):
        total += jnp.dot(gathered[k], mixing_ref[k], preferred_element_type=F32)
    return total


def edge_kernel(
    fields_ref, left_ref, right_ref, stencil_ref, reach_ref, up_ref, down_ref, taps_ref
):
    place_taps(stencil_ref, reach_ref, taps_ref, 48)
    for out_ref, first, line in ((up_ref, A - EDGE, A - RLAT), (down_ref, 0, 0)):
        for a in range(EDGE):
            for n, part in enumerate((left_ref, fields_ref, right_ref)):
                out_ref[48 * a + 16 * n : 48 * a + 16 * n + 16, :] = part[first + a]
        lines = [taps_ref[k, line : line + RLAT, :] for k in range(KB)]
        lines = jnp.concatenate(lines + [jnp.zeros((16 - KB * RLAT, LANES), F32)], axis=0)
        lines = jnp.concatenate([lines, jnp.zeros((16, C - LANES), F32)], axis=1)
        out_ref[48 * EDGE : 48 * EDGE + 16, :] = lines.astype(BF)


def first_kernel(
    fields_ref, left_ref, right_ref, above_ref, below_ref, taps_ref, mix_ref, out_ref,
    field, taps, gathered,
):
    field[: 48 * EDGE, :] = above_ref[: 48 * EDGE, :]
    field[48 * (A + EDGE) :, :] = below_ref[: 48 * EDGE, :]
    for a in range(A):
        for n, part in enumerate((left_ref, fields_ref, right_ref)):
            at = 48 * (a + EDGE) + 16 * n
            field[at : at + 16, :] = part[a]
    top = above_ref[48 * EDGE : 48 * EDGE + 16, :].astype(F32)
    bottom = below_ref[48 * EDGE : 48 * EDGE + 16, :].astype(F32)
    for k in range(KB):
        part = slice(RLAT * k, RLAT * k + RLAT)
        taps[k, :RLAT, :] = top[part, :LANES]
        taps[k, RLAT : RLAT + A, :] = taps_ref[k]
        taps[k, RLAT + A : AX, :] = bottom[part, :LANES]
    first = gather_rows(taps, field, mix_ref, gathered, AX, JX, 48, 16 - OFF - RLON)
    for a in range(AX):
        own = field[(a + RLAT) * 48 : (a + RLAT) * 48 + 48, :].astype(F32)
        out_ref[a * JX : (a + 1) * JX, :] = (
            first[a * JX : (a + 1) * JX] + own[16 - OFF : 16 - OFF + JX]
        )


def lines_kernel(stencil_ref, reach_ref, taps_ref):
    place_taps(stencil_ref, reach_ref, taps_ref, JX)


def last_kernel(
    place_ref, recv_ref, pre_ref, taps_ref, norm_ref, mix_ref, in_ref, back_ref, out_ref,
    rows, stream, exact, gathered,
):
    place = place_ref[0]
    for s in range(PLON):
        rows[60 * s : 60 * s + 60, :] = recv_ref[s].astype(F32)
    for hi in range(5):
        spectral = rows[pl.ds(hi, C, stride=5), :].T
        value = pre_ref[128 * hi : 128 * hi + 128, :] + spectral
        row = lax.broadcasted_iota(jnp.int32, (128, C), 0) // JX + 4 * hi - RLAT + place * A
        value = jnp.where((row >= 0) & (row < NLAT), value, 0.0).astype(BF)
        stream[128 * hi : 128 * hi + 128, :] = value
        exact[128 * hi : 128 * hi + 128, :] = value.astype(F32)
    second = gather_rows(taps_ref, stream, mix_ref, gathered, A, N, JX, OFF - RLON)
    own = jnp.concatenate(
        [exact[(a + RLAT) * JX + OFF : (a + RLAT) * JX + OFF + N, :] for a in range(A)], axis=0
    )
    summed = own + second
    center = summed - jnp.mean(summed, axis=-1, keepdims=True)
    spread = jnp.mean(center * center, axis=-1, keepdims=True)
    normed = (center * lax.rsqrt(spread + 1e-05) * norm_ref[...]).astype(BF)
    hidden = jax.nn.gelu(jnp.dot(normed, in_ref[...], preferred_element_type=F32)).astype(BF)
    update = jnp.dot(hidden, back_ref[...], preferred_element_type=F32)
    out_ref[...] = (own + update).astype(BF).reshape(A, N, C)


def legendre_start(colatitude, orders, degrees):
    order_vals = orders.astype(F32)
    counter = jnp.arange(1, degrees + 1, dtype=jnp.int32).astype(F32)
    factors = jnp.log((2.0 * counter - 1.0) / (2.0 * counter))
    partial_sum = jnp.sum(
        jnp.where(counter[None, :] <= order_vals[:, None], factors[None, :], 0.0), axis=1
    )
    log_sine = jnp.log(jnp.sin(colatitude))
    start_log = 0.5 * jnp.log((2.0 * order_vals + 1.0) / (4.0 * math.pi)) + 0.5 * partial_sum
    return jnp.exp(start_log[:, None] + order_vals[:, None] * log_sine[None, :])


def shifted(value, axis, by, closed):
    count = lax.axis_size(axis)
    pairs = [(i, (i + by) % count) for i in range(count) if closed or 0 <= i + by < count]
    return lax.ppermute(value, axis, pairs)


def exchange(block, axis):
    return lax.all_to_all(block, axis, split_axis=0, concat_axis=0, tiled=True)


def shape(dims, dtype):
    return jax.ShapeDtypeStruct(dims, dtype)


def local(
    fields, spectral_gain, stencil_one, stencil_two, cycle_reach, mix_one, mix_two, norm_gain,
    w_in, w_out,
):
    place = lax.axis_index("lat")
    colatitude = math.pi * (jnp.arange(NLAT, dtype=jnp.int32).astype(F32) + 0.5) / NLAT
    quad = math.pi / NLAT * (2.0 * math.pi / NLON) * jnp.sin(colatitude)
    own_orders = place * ML + jnp.minimum(jnp.arange(CP, dtype=jnp.int32), ML - 1)
    diagonal = legendre_start(colatitude, own_orders, M)

    sent = call(
        prep_kernel,
        shape((PLON, 24, 128), BF),
        [
            pltpu.VMEM((3, A, N, 128), BF),
            pltpu.VMEM((768, 128), F32),
            pltpu.SemaphoreType.DMA((3,)),
        ],
        fields,
        hbm=(0,),
        limit=LAST_LIMIT,
        moved=1.1,
    )
    sent, late_place, own_fields = lax.optimization_barrier((sent, place.reshape(1), fields))
    recv = exchange(sent, "lon")
    left = shifted(own_fields, "lon", 1, True)
    right = shifted(own_fields, "lon", -1, True)
    factors = call(
        twiddle_kernel,
        [
            shape((rows, 2 * M), F32)
            for rows in (PLON, PLON, N, N, PLON, PLON, JX, JX)
        ],
        [],
        late_place,
        smem=(0,),
        moved=0.4,
    )

    def by_offset(stencil):
        return jnp.transpose(stencil, (1, 2, 0, 3)).reshape(KB * DLAT, A, TAPS)

    spectra = call(
        forward_kernel,
        shape((PLAT, 48, 128), BF),
        [pltpu.VMEM((4, 256, 128), F32), pltpu.VMEM((768, 128), F32)],
        recv,
        *factors[:4],
        moved=1.4,
    )
    spectra, late_orders, left, right = lax.optimization_barrier(
        (spectra, own_orders, left, right)
    )
    gathered = exchange(spectra, "lat")
    table = call(
        table_kernel,
        shape((ML, M, NLAT), BF),
        [pltpu.VMEM((2, M * CP, 128), F32)],
        jnp.broadcast_to(late_orders.astype(F32)[:, None], (CP, 128)),
        jnp.cos(colatitude)[None, :],
        diagonal,
        moved=3.3,
    )
    up, down, taps_one = call(
        edge_kernel,
        [shape((48 * EDGE + 16, C), BF)] * 2 + [shape((KB, A, LANES), F32)],
        [],
        own_fields,
        left,
        right,
        by_offset(stencil_one),
        cycle_reach,
        smem=(4,),
        moved=0.7,
    )
    gathered, up, down = lax.optimization_barrier((gathered, up, down))
    gain = jnp.pad(spectral_gain.T, ((0, CP - CL), (0, 0)))
    results = call(
        legendre_kernel,
        shape((PLAT, 48, 128), BF),
        [pltpu.VMEM((2, 384, 128), F32), pltpu.VMEM((2, 288, 128), F32)],
        gathered,
        table,
        quad[None, :],
        jnp.concatenate([gain, gain], axis=0),
        moved=2.6,
    )
    results, up, down = lax.optimization_barrier((results, up, down))
    returned = exchange(results, "lat")
    above = shifted(up, "lat", 1, False)
    below = shifted(down, "lat", -1, False)
    returned, above, below = lax.optimization_barrier((returned, above, below))
    sectors = call(
        inverse_kernel,
        shape((PLON, 60, 128), BF),
        [
            pltpu.VMEM((768, 128), F32),
            pltpu.VMEM((CL * AX, 2 * M), F32),
            pltpu.VMEM((8, CL * AX, 128), F32),
        ],
        returned,
        *factors[4:],
        moved=1.7,
    )
    spectral = exchange(sectors, "lon")

    pre = call(
        first_kernel,
        shape((AX * JX, C), F32),
        [
            pltpu.VMEM(((AX + EDGE) * 48, C), BF),
            pltpu.VMEM((KB, 24, LANES), F32),
            pltpu.VMEM((KB, AX * JX, C), BF),
        ],
        own_fields,
        left,
        right,
        above,
        below,
        taps_one,
        mix_one,
        moved=1.9,
    )
    pre, late_two = lax.optimization_barrier((pre, by_offset(stencil_two)))
    taps_two = call(
        lines_kernel,
        shape((KB, A, LANES), F32),
        [],
        late_two,
        cycle_reach,
        smem=(1,),
        moved=8.0,
    )
    return call(
        last_kernel,
        shape((A, N, C), BF),
        [
            pltpu.VMEM((1920, 128), F32),
            pltpu.VMEM((AX * JX, C), BF),
            pltpu.VMEM((AX * JX, C), F32),
            pltpu.VMEM((KB, A * N, C), BF),
        ],
        place.reshape(1),
        spectral,
        pre,
        taps_two,
        norm_gain[None, :],
        mix_two,
        w_in,
        w_out,
        smem=(0,),
        moved=2.7,
    )


def solution(mesh):
    in_specs = (
        P("lat", "lon", None),
        P(None, "lon"),
        P("lat", None, None, None),
        P("lat", None, None, None),
        P("lat"),
        P(),
        P(),
        P(),
        P(),
        P(),
    )
    out_specs = P("lat", "lon", None)
    return jax.shard_map(local, mesh=mesh, in_specs=in_specs, out_specs=out_specs, check_vma=False)
```

```python
import functools
import math

import jax
import jax.numpy as jnp
from jax import lax
from jax.experimental import pallas as pl
from jax.experimental.pallas import tpu as pltpu
from jax.sharding import PartitionSpec as P

C = 384
CL = 12
CP = 16
KB = 3
RLAT = 2
RLON = 6
TAPS = 2 * RLON + 1
DLAT = 2 * RLAT + 1
NLAT = 256
NLON = 512
PLAT = 16
PLON = 32
A = 16
N = 16
M = 192
ML = 12
AX = A + 2 * RLAT
JX = 32
OFF = 8
LANES = 256
EDGE = 2 * RLAT
HALO = 2 * RLON
F32 = jnp.float32
BF = jnp.bfloat16
NT = (((1,), (1,)), ((), ()))
VMEM_LIMIT = 14 * 1024 * 1024
LAST_LIMIT = 61 * 1024 * 1024


def call(kernel, outs, scratch, *args, smem=(), hbm=(), limit=VMEM_LIMIT, moved=1.0):
    specs = [
        pl.BlockSpec(
            memory_space=pltpu.SMEM if i in smem else pltpu.HBM if i in hbm else pltpu.VMEM
        )
        for i in range(len(args))
    ]
    out_specs = jax.tree.map(lambda _: pl.BlockSpec(memory_space=pltpu.VMEM), outs)
    return pl.pallas_call(
        kernel,
        out_shape=outs,
        in_specs=specs,
        out_specs=out_specs,
        scratch_shapes=scratch,
        cost_estimate=pl.CostEstimate(
            flops=int(moved * 500_000_000), bytes_accessed=int(moved * 3_400_000), transcendentals=0
        ),
        compiler_params=pltpu.CompilerParams(vmem_limit_bytes=limit),
    )(*args)


def swap_blocks(pieces, width):
    count = len(pieces)
    pieces = list(pieces)
    block = lax.broadcasted_iota(jnp.int32, pieces[0].shape, 1) // width
    step = 1
    while step < count:
        low = (block & step) == 0
        for i in range(count):
            if i & step:
                continue
            x, y = pieces[i], pieces[i | step]
            pieces[i] = jnp.where(low, x, pltpu.roll(y, step * width, 1))
            pieces[i | step] = jnp.where(low, pltpu.roll(x, 128 - step * width, 1), y)
        step *= 2
    return pieces


def prep_kernel(fields_ref, out_ref, field, rows, sems):
    copies = [
        pltpu.make_async_copy(
            fields_ref.at[:, :, pl.ds(128 * g, 128)], field.at[g], sems.at[g]
        )
        for g in range(3)
    ]
    for copy in copies:
        copy.start()
    for g in range(3):
        copies[g].wait()
        turned = field[g].reshape(A * N, 128).astype(F32).T
        for hi in range(2):
            rows[pl.ds(256 * g + hi, 128, stride=2), :] = turned[:, hi * 128 : hi * 128 + 128]
    for d in range(PLON):
        out_ref[d] = rows[24 * d : 24 * d + 24, :].astype(BF)


def twiddle_kernel(place_ref, u_ref, v_ref, c_ref, s_ref, iu_ref, iv_ref, ic_ref, is_ref):
    lane = lax.broadcasted_iota(jnp.int32, (PLON, 2 * M), 1)
    row = lax.broadcasted_iota(jnp.int32, (PLON, 2 * M), 0)
    order = lane // 2

    def turn(product):
        return 2.0 * math.pi / NLON * (product & (NLON - 1)).astype(F32)

    outer = turn(row * N * order + (lane & 1) * (NLON // 4))
    cos, sin = jnp.cos(outer), -jnp.sin(outer)
    scale = jnp.where(order == 0, 1.0, 2.0)
    u_ref[...], v_ref[...] = cos, sin
    iu_ref[...], iv_ref[...] = cos * scale, sin * scale
    inner = turn((row - OFF) * order)
    cos, sin = jnp.cos(inner), jnp.sin(inner)
    ic_ref[...], is_ref[...] = cos, sin
    c_ref[...], s_ref[...] = cos[OFF : OFF + N], sin[OFF : OFF + N]


def place_taps(stencil_ref, reach_ref, out_ref, wide):
    offset = lax.broadcasted_iota(jnp.int32, (A, TAPS), 1) - RLON
    cycle = lax.broadcasted_iota(jnp.int32, (A, TAPS), 0)
    reach = jnp.zeros((A, TAPS), jnp.int32)
    for a in range(A):
        reach = jnp.where(cycle == a, reach_ref[a], reach)
    inside = jnp.abs(offset) <= reach
    for k in range(KB):
        total = None
        for d in range(DLAT):
            taps = jnp.where(inside, stencil_ref[k * DLAT + d].astype(F32), 0.0)
            taps = jnp.concatenate([taps, jnp.zeros((A, LANES - TAPS), F32)], axis=1)
            taps = pltpu.roll(taps, d * wide, 1) if d else taps
            total = taps if total is None else total + taps
        out_ref[k] = total


def table_kernel(
    order_ref, cos_ref, diag_ref, out_ref, rows
):
    order = order_ref[...]
    square = order * order
    cosine = [jnp.broadcast_to(cos_ref[:, h * 128 : h * 128 + 128], (CP, 128)) for h in range(2)]
    diag = [diag_ref[:, h * 128 : h * 128 + 128] for h in range(2)]
    zero = order * 0.0

    def step(degree, state):
        deg = jnp.full((CP, 128), degree, jnp.int32).astype(F32)
        back = deg - 1.0
        up = jnp.sqrt(jnp.maximum(4.0 * deg * deg - 1.0, 0.0) / jnp.maximum(deg * deg - square, 1.0))
        down = jnp.sqrt(
            jnp.maximum(back * back - square, 0.0) / jnp.maximum(4.0 * back * back - 1.0, 1.0)
        )
        new = []
        for h in range(2):
            previous, earlier = state[2 * h], state[2 * h + 1]
            entry = (up * cosine[h]) * previous - (up * down) * earlier
            entry = jnp.where(order == deg, diag[h], entry)
            rows[h, pl.ds(pl.multiple_of(degree * CP, CP), CP), :] = entry
            new += [entry, previous]
        return tuple(new)

    lax.fori_loop(0, M, step, (zero,) * 4, unroll=8)
    for m in range(ML):
        for h in range(2):
            out_ref[m, :, h * 128 : h * 128 + 128] = rows.at[h][
                pl.ds(m, M, stride=CP), :
            ].astype(BF)


def forward_kernel(recv_ref, u_ref, v_ref, c_ref, s_ref, out_ref, grid, rows):
    pieces = [
        jnp.concatenate([recv_ref[hi * 8 + lo].astype(F32) for hi in range(4)], axis=0)
        for lo in range(8)
    ]
    pieces = swap_blocks(pieces, 16)
    for hi in range(4):
        for lo in range(8):
            grid.at[hi][pl.ds(lo, 24, stride=8), :] = pieces[lo][hi * 24 : hi * 24 + 24]
        grid[hi, 192:256, :] = jnp.zeros((64, 128), F32)
    circles = jnp.concatenate([grid[hi].astype(BF) for hi in range(4)], axis=1)
    cosb, sinb = c_ref[...], s_ref[...]
    table = jnp.concatenate(
        [
            (u_ref[s : s + 1, :] * cosb + v_ref[s : s + 1, :] * sinb).astype(BF)
            for s in range(PLON)
        ],
        axis=0,
    )
    spectra = jnp.dot(circles, table, preferred_element_type=F32).T
    for g in range(2):
        rows[pl.ds(g, 2 * M, stride=2), :] = spectra[:, g * 128 : g * 128 + 128]
    for e in range(PLAT):
        out_ref[e] = rows[48 * e : 48 * e + 48, :].astype(BF)


def split(value):
    high = value.astype(BF)
    low = (value - high.astype(F32)).astype(BF)
    return jnp.concatenate([high, low], axis=0)


def legendre_kernel(recv_ref, tab_ref, quad_ref, gain_ref, out_ref, grid, res):
    pieces = [
        jnp.concatenate([recv_ref[hi * 8 + lo].astype(F32) for hi in range(2)], axis=0)
        for lo in range(8)
    ]
    pieces = swap_blocks(pieces, 16)
    for hi in range(2):
        for x in range(8):
            grid.at[hi][pl.ds(x, 48, stride=8), :] = pieces[x][hi * 48 : hi * 48 + 48]
    gain = gain_ref[...]
    quad = quad_ref[...]
    for m in range(ML):
        part = slice(32 * m, 32 * m + 32)
        weighted = jnp.concatenate([grid[0, part, :], grid[1, part, :]], axis=1) * quad
        table = tab_ref[m]
        both = lax.dot_general(split(weighted), table, NT, preferred_element_type=F32)
        harmonics = (both[:32] + both[32:]) * gain
        both = jnp.dot(split(harmonics), table, preferred_element_type=F32)
        result = both[:32] + both[32:]
        for r in range(2):
            at = (2 * m + r) * CL
            for h in range(2):
                res[h, at : at + CL, :] = result[16 * r : 16 * r + CL, h * 128 : h * 128 + 128]
    lanes = lax.broadcasted_iota(jnp.int32, (48, 128), 1)
    source = [[res.at[h][pl.ds(lo, 48, stride=6), :] for lo in range(6)] for h in range(2)]
    for j in range(PLAT):
        total = None
        for lo in range(6):
            shift = (lo * AX - (16 * j - RLAT)) % 128
            value = pltpu.roll(source[j // 8][lo], shift, 1) if shift else source[j // 8][lo]
            if j in (7, 8):
                other = source[1 - j // 8][lo]
                other = pltpu.roll(other, shift, 1) if shift else other
                bound = 128 - (16 * 7 - RLAT) if j == 7 else RLAT
                first, last = (value, other) if j == 7 else (other, value)
                value = jnp.where(lanes < lo * AX + bound, first, last)
            total = value if total is None else jnp.where(lanes >= lo * AX, value, total)
        out_ref[j] = total.astype(BF)


def inverse_kernel(recv_ref, u_ref, v_ref, c_ref, s_ref, out_ref, rows, coef, grid):
    for e in range(PLAT):
        rows[48 * e : 48 * e + 48, :] = recv_ref[e].astype(F32)
    for hi in range(2):
        turned = rows[pl.ds(hi, 2 * M, stride=2), :].T
        coef[hi * 6 * AX : (hi + 1) * 6 * AX, :] = turned[: 6 * AX, :]
    left = coef[...].astype(BF)
    cosb, sinb = c_ref[...], s_ref[...]
    for k in range(8):
        table = jnp.concatenate(
            [
                (u_ref[d : d + 1, :] * cosb + v_ref[d : d + 1, :] * sinb).astype(BF)
                for d in range(4 * k, 4 * k + 4)
            ],
            axis=0,
        )
        grid[k] = lax.dot_general(left, table, NT, preferred_element_type=F32)
    for k in range(8):
        pieces = [grid.at[k][pl.ds(lo, 60, stride=4), :] for lo in range(4)]
        pieces = swap_blocks(pieces, 32)
        for lo in range(4):
            out_ref[4 * k + lo] = pieces[lo].astype(BF)


def gather_rows(taps_ref, field, mixing_ref, gathered, rows, cols, wide, start):
    for a in range(rows):
        bands = []
        for k in range(KB):
            line = taps_ref[k, a : a + 1, :]
            band = pltpu.roll(
                jnp.broadcast_to(line, (cols, LANES)), start, 1, stride=1, stride_axis=0
            )
            bands.append(band.astype(BF))
        band = jnp.concatenate(bands, axis=0)[:, : DLAT * wide]
        value = jnp.dot(
            band, field[a * wide : (a + DLAT) * wide, :], preferred_element_type=F32
        ).astype(BF)
        for k in range(KB):
            gathered[k, a * cols : (a + 1) * cols, :] = value[k * cols : (k + 1) * cols]
    total = jnp.dot(gathered[0], mixing_ref[0], preferred_element_type=F32)
    for k in range(1, KB):
        total += jnp.dot(gathered[k], mixing_ref[k], preferred_element_type=F32)
    return total


def edge_kernel(fields_ref, stencil_ref, reach_ref, up_ref, down_ref, taps_ref):
    place_taps(stencil_ref, reach_ref, taps_ref, 48)
    for out_ref, first, line in ((up_ref, A - EDGE, A - RLAT), (down_ref, 0, 0)):
        for a in range(EDGE):
            out_ref[N * a : N * a + N, :] = fields_ref[first + a]
        lines = [taps_ref[k, line : line + RLAT, :] for k in range(KB)]
        lines = jnp.concatenate(lines + [jnp.zeros((N - KB * RLAT, LANES), F32)], axis=0)
        lines = jnp.concatenate([lines, jnp.zeros((N, C - LANES), F32)], axis=1)
        out_ref[N * EDGE : N * EDGE + N, :] = lines.astype(BF)


def rim_row(a, fields_ref, above_ref, below_ref):
    if a < EDGE:
        return above_ref[N * a : N * a + N, :]
    if a < A + EDGE:
        return fields_ref[a - EDGE]
    return below_ref[N * (a - A - EDGE) : N * (a - A - EDGE) + N, :]


def rim_kernel(fields_ref, above_ref, below_ref, left_ref, right_ref, ahead, behind):
    for a in range(AX + EDGE):
        row = rim_row(a, fields_ref, above_ref, below_ref).astype(F32)
        ahead[HALO * a : HALO * a + HALO, :] = row[N - HALO :]
        behind[HALO * a : HALO * a + HALO, :] = row[:HALO]
    right_ref[...] = ahead[...].astype(BF)
    left_ref[...] = behind[...].astype(BF)


def first_kernel(
    fields_ref, left_ref, right_ref, above_ref, below_ref, taps_ref, mix_ref, out_ref,
    field, taps, gathered, before, after,
):
    before[...] = left_ref[...].astype(F32)
    after[...] = right_ref[...].astype(F32)
    gap = jnp.zeros((N - HALO, C), F32)
    for a in range(AX + EDGE):
        part = slice(HALO * a, HALO * a + HALO)
        own = rim_row(a, fields_ref, above_ref, below_ref).astype(F32)
        row = jnp.concatenate([gap, before[part, :], own, after[part, :], gap], axis=0)
        field[48 * a : 48 * a + 48, :] = row.astype(BF)
    top = above_ref[N * EDGE : N * EDGE + N, :].astype(F32)
    bottom = below_ref[N * EDGE : N * EDGE + N, :].astype(F32)
    for k in range(KB):
        part = slice(RLAT * k, RLAT * k + RLAT)
        taps[k, :RLAT, :] = top[part, :LANES]
        taps[k, RLAT : RLAT + A, :] = taps_ref[k]
        taps[k, RLAT + A : AX, :] = bottom[part, :LANES]
    first = gather_rows(taps, field, mix_ref, gathered, AX, JX, 48, 16 - OFF - RLON)
    for a in range(AX):
        own = field[(a + RLAT) * 48 : (a + RLAT) * 48 + 48, :].astype(F32)
        value = first[a * JX : (a + 1) * JX] + own[16 - OFF : 16 - OFF + JX]
        out_ref[a * JX : (a + 1) * JX, :] = value.astype(BF)


def lines_kernel(stencil_ref, reach_ref, taps_ref):
    place_taps(stencil_ref, reach_ref, taps_ref, JX)


def last_kernel(
    place_ref, recv_ref, pre_ref, taps_ref, norm_ref, mix_ref, in_ref, back_ref, out_ref,
    rows, stream, exact, gathered,
):
    place = place_ref[0]
    for s in range(PLON):
        rows[60 * s : 60 * s + 60, :] = recv_ref[s].astype(F32)
    for hi in range(5):
        spectral = rows[pl.ds(hi, C, stride=5), :].T
        value = pre_ref[128 * hi : 128 * hi + 128, :].astype(F32) + spectral
        row = lax.broadcasted_iota(jnp.int32, (128, C), 0) // JX + 4 * hi - RLAT + place * A
        value = jnp.where((row >= 0) & (row < NLAT), value, 0.0).astype(BF)
        stream[128 * hi : 128 * hi + 128, :] = value
        exact[128 * hi : 128 * hi + 128, :] = value.astype(F32)
    second = gather_rows(taps_ref, stream, mix_ref, gathered, A, N, JX, OFF - RLON)
    own = jnp.concatenate(
        [exact[(a + RLAT) * JX + OFF : (a + RLAT) * JX + OFF + N, :] for a in range(A)], axis=0
    )
    summed = own + second
    center = summed - jnp.mean(summed, axis=-1, keepdims=True)
    spread = jnp.mean(center * center, axis=-1, keepdims=True)
    normed = (center * lax.rsqrt(spread + 1e-05) * norm_ref[...]).astype(BF)
    hidden = jax.nn.gelu(jnp.dot(normed, in_ref[...], preferred_element_type=F32)).astype(BF)
    update = jnp.dot(hidden, back_ref[...], preferred_element_type=F32)
    out_ref[...] = (own + update).astype(BF).reshape(A, N, C)


def legendre_start(colatitude, orders, degrees):
    order_vals = orders.astype(F32)
    counter = jnp.arange(1, degrees + 1, dtype=jnp.int32).astype(F32)
    factors = jnp.log((2.0 * counter - 1.0) / (2.0 * counter))
    partial_sum = jnp.sum(
        jnp.where(counter[None, :] <= order_vals[:, None], factors[None, :], 0.0), axis=1
    )
    log_sine = jnp.log(jnp.sin(colatitude))
    start_log = 0.5 * jnp.log((2.0 * order_vals + 1.0) / (4.0 * math.pi)) + 0.5 * partial_sum
    return jnp.exp(start_log[:, None] + order_vals[:, None] * log_sine[None, :])


def shifted(value, axis, by, closed):
    count = lax.axis_size(axis)
    pairs = [(i, (i + by) % count) for i in range(count) if closed or 0 <= i + by < count]
    return lax.ppermute(value, axis, pairs)


def exchange(block, axis):
    return lax.all_to_all(block, axis, split_axis=0, concat_axis=0, tiled=True)


def shape(dims, dtype):
    return jax.ShapeDtypeStruct(dims, dtype)


def local(
    fields, spectral_gain, stencil_one, stencil_two, cycle_reach, mix_one, mix_two, norm_gain,
    w_in, w_out,
):
    place = lax.axis_index("lat")
    colatitude = math.pi * (jnp.arange(NLAT, dtype=jnp.int32).astype(F32) + 0.5) / NLAT
    quad = math.pi / NLAT * (2.0 * math.pi / NLON) * jnp.sin(colatitude)
    own_orders = place * ML + jnp.minimum(jnp.arange(CP, dtype=jnp.int32), ML - 1)
    diagonal = legendre_start(colatitude, own_orders, M)

    sent = call(
        prep_kernel,
        shape((PLON, 24, 128), BF),
        [
            pltpu.VMEM((3, A, N, 128), BF),
            pltpu.VMEM((768, 128), F32),
            pltpu.SemaphoreType.DMA((3,)),
        ],
        fields,
        hbm=(0,),
        limit=LAST_LIMIT,
        moved=1.1,
    )
    sent, late_place, late_orders = lax.optimization_barrier(
        (sent, place.reshape(1), own_orders)
    )
    recv = exchange(sent, "lon")
    factors = call(
        twiddle_kernel,
        [
            shape((rows, 2 * M), F32)
            for rows in (PLON, PLON, N, N, PLON, PLON, JX, JX)
        ],
        [],
        late_place,
        smem=(0,),
        moved=0.4,
    )

    def by_offset(stencil):
        return jnp.transpose(stencil, (1, 2, 0, 3)).reshape(KB * DLAT, A, TAPS)

    table = call(
        table_kernel,
        shape((ML, M, NLAT), BF),
        [pltpu.VMEM((2, M * CP, 128), F32)],
        jnp.broadcast_to(late_orders.astype(F32)[:, None], (CP, 128)),
        jnp.cos(colatitude)[None, :],
        diagonal,
        moved=3.3,
    )
    recv, table = lax.optimization_barrier((recv, table))
    spectra = call(
        forward_kernel,
        shape((PLAT, 48, 128), BF),
        [pltpu.VMEM((4, 256, 128), F32), pltpu.VMEM((768, 128), F32)],
        recv,
        *factors[:4],
        moved=1.4,
    )
    up, down, taps_one = call(
        edge_kernel,
        [shape((N * EDGE + N, C), BF)] * 2 + [shape((KB, A, LANES), F32)],
        [],
        fields,
        by_offset(stencil_one),
        cycle_reach,
        smem=(2,),
        moved=0.7,
    )
    spectra, up, down = lax.optimization_barrier((spectra, up, down))
    gathered = exchange(spectra, "lat")
    above = shifted(up, "lat", 1, False)
    below = shifted(down, "lat", -1, False)
    gain = jnp.pad(spectral_gain.T, ((0, CP - CL), (0, 0)))
    results = call(
        legendre_kernel,
        shape((PLAT, 48, 128), BF),
        [pltpu.VMEM((2, 384, 128), F32), pltpu.VMEM((2, 288, 128), F32)],
        gathered,
        table,
        quad[None, :],
        jnp.concatenate([gain, gain], axis=0),
        moved=2.6,
    )
    results, above, below = lax.optimization_barrier((results, above, below))
    returned = exchange(results, "lat")
    to_left, to_right = call(
        rim_kernel,
        [shape((HALO * (AX + EDGE), C), BF)] * 2,
        [pltpu.VMEM((HALO * (AX + EDGE), C), F32)] * 2,
        fields,
        above,
        below,
        moved=0.5,
    )
    left = shifted(to_right, "lon", 1, True)
    right = shifted(to_left, "lon", -1, True)
    sectors = call(
        inverse_kernel,
        shape((PLON, 60, 128), BF),
        [
            pltpu.VMEM((768, 128), F32),
            pltpu.VMEM((CL * AX, 2 * M), F32),
            pltpu.VMEM((8, CL * AX, 128), F32),
        ],
        returned,
        *factors[4:],
        moved=1.7,
    )
    spectral = exchange(sectors, "lon")
    pre = call(
        first_kernel,
        shape((AX * JX, C), BF),
        [
            pltpu.VMEM(((AX + EDGE) * 48, C), BF),
            pltpu.VMEM((KB, 24, LANES), F32),
            pltpu.VMEM((KB, AX * JX, C), BF),
            pltpu.VMEM((HALO * (AX + EDGE), C), F32),
            pltpu.VMEM((HALO * (AX + EDGE), C), F32),
        ],
        fields,
        left,
        right,
        above,
        below,
        taps_one,
        mix_one,
        moved=0.1,
    )
    pre, late_two = lax.optimization_barrier((pre, by_offset(stencil_two)))
    taps_two = call(
        lines_kernel,
        shape((KB, A, LANES), F32),
        [],
        late_two,
        cycle_reach,
        smem=(1,),
        moved=20.0,
    )
    return call(
        last_kernel,
        shape((A, N, C), BF),
        [
            pltpu.VMEM((1920, 128), F32),
            pltpu.VMEM((AX * JX, C), BF),
            pltpu.VMEM((AX * JX, C), F32),
            pltpu.VMEM((KB, A * N, C), BF),
        ],
        place.reshape(1),
        spectral,
        pre,
        taps_two,
        norm_gain[None, :],
        mix_two,
        w_in,
        w_out,
        smem=(0,),
        moved=2.7,
    )


def solution(mesh):
    in_specs = (
        P("lat", "lon", None),
        P(None, "lon"),
        P("lat", None, None, None),
        P("lat", None, None, None),
        P("lat"),
        P(),
        P(),
        P(),
        P(),
        P(),
    )
    out_specs = P("lat", "lon", None)
    return jax.shard_map(local, mesh=mesh, in_specs=in_specs, out_specs=out_specs, check_vma=False)
```

```python
import functools
import math

import jax
import jax.numpy as jnp
from jax import lax
from jax.experimental import pallas as pl
from jax.experimental.pallas import tpu as pltpu
from jax.sharding import PartitionSpec as P

C = 384
CL = 12
CP = 16
KB = 3
RLAT = 2
RLON = 6
TAPS = 2 * RLON + 1
DLAT = 2 * RLAT + 1
NLAT = 256
NLON = 512
PLAT = 16
PLON = 32
A = 16
N = 16
M = 192
ML = 12
AX = A + 2 * RLAT
JX = 32
OFF = 8
LANES = 256
EDGE = 2 * RLAT
HALO = 2 * RLON
F32 = jnp.float32
BF = jnp.bfloat16
NT = (((1,), (1,)), ((), ()))
VMEM_LIMIT = 14 * 1024 * 1024
LAST_LIMIT = 61 * 1024 * 1024


def call(kernel, outs, scratch, *args, smem=(), hbm=(), out=pltpu.VMEM, limit=VMEM_LIMIT, moved=1.0):
    specs = [
        pl.BlockSpec(
            memory_space=pltpu.SMEM if i in smem else pltpu.HBM if i in hbm else pltpu.VMEM
        )
        for i in range(len(args))
    ]
    out_specs = jax.tree.map(lambda _: pl.BlockSpec(memory_space=out), outs)
    return pl.pallas_call(
        kernel,
        out_shape=outs,
        in_specs=specs,
        out_specs=out_specs,
        scratch_shapes=scratch,
        cost_estimate=pl.CostEstimate(
            flops=int(moved * 500_000_000), bytes_accessed=int(moved * 3_400_000), transcendentals=0
        ),
        compiler_params=pltpu.CompilerParams(vmem_limit_bytes=limit),
    )(*args)


def swap_blocks(pieces, width):
    count = len(pieces)
    pieces = list(pieces)
    block = lax.broadcasted_iota(jnp.int32, pieces[0].shape, 1) // width
    step = 1
    while step < count:
        low = (block & step) == 0
        for i in range(count):
            if i & step:
                continue
            x, y = pieces[i], pieces[i | step]
            pieces[i] = jnp.where(low, x, pltpu.roll(y, step * width, 1))
            pieces[i | step] = jnp.where(low, pltpu.roll(x, 128 - step * width, 1), y)
        step *= 2
    return pieces


def send(stage, out_ref, sems, number, first, count):
    part = pl.ds(first, count)
    copy = pltpu.make_async_copy(stage.at[part], out_ref.at[part], sems.at[number])
    copy.start()
    return copy


def prep_kernel(fields_ref, out_ref, field, rows, sems, stage, out_sems):
    copies = [
        pltpu.make_async_copy(
            fields_ref.at[:, :, pl.ds(128 * g, 128)], field.at[g], sems.at[g]
        )
        for g in range(3)
    ]
    for copy in copies:
        copy.start()
    for g in range(3):
        copies[g].wait()
        turned = field[g].reshape(A * N, 128).astype(F32).T
        for hi in range(2):
            rows[pl.ds(256 * g + hi, 128, stride=2), :] = turned[:, hi * 128 : hi * 128 + 128]
        first, last = ((0, 10), (10, 21), (21, PLON))[g]
        for d in range(first, last):
            stage[d] = rows[24 * d : 24 * d + 24, :].astype(BF)
        copies.append(send(stage, out_ref, out_sems, g, first, last - first))
    for copy in copies[3:]:
        copy.wait()


def twiddle_kernel(place_ref, u_ref, v_ref, c_ref, s_ref, iu_ref, iv_ref, ic_ref, is_ref):
    lane = lax.broadcasted_iota(jnp.int32, (PLON, 2 * M), 1)
    row = lax.broadcasted_iota(jnp.int32, (PLON, 2 * M), 0)
    order = lane // 2

    def turn(product):
        return 2.0 * math.pi / NLON * (product & (NLON - 1)).astype(F32)

    outer = turn(row * N * order + (lane & 1) * (NLON // 4))
    cos, sin = jnp.cos(outer), -jnp.sin(outer)
    scale = jnp.where(order == 0, 1.0, 2.0)
    u_ref[...], v_ref[...] = cos, sin
    iu_ref[...], iv_ref[...] = cos * scale, sin * scale
    inner = turn((row - OFF) * order)
    cos, sin = jnp.cos(inner), jnp.sin(inner)
    ic_ref[...], is_ref[...] = cos, sin
    c_ref[...], s_ref[...] = cos[OFF : OFF + N], sin[OFF : OFF + N]


def place_taps(stencil_ref, reach_ref, out_ref, wide):
    offset = lax.broadcasted_iota(jnp.int32, (A, TAPS), 1) - RLON
    cycle = lax.broadcasted_iota(jnp.int32, (A, TAPS), 0)
    reach = jnp.zeros((A, TAPS), jnp.int32)
    for a in range(A):
        reach = jnp.where(cycle == a, reach_ref[a], reach)
    inside = jnp.abs(offset) <= reach
    for k in range(KB):
        total = None
        for d in range(DLAT):
            taps = jnp.where(inside, stencil_ref[k * DLAT + d].astype(F32), 0.0)
            taps = jnp.concatenate([taps, jnp.zeros((A, LANES - TAPS), F32)], axis=1)
            taps = pltpu.roll(taps, d * wide, 1) if d else taps
            total = taps if total is None else total + taps
        out_ref[k] = total


def table_kernel(
    order_ref, cos_ref, diag_ref, out_ref, rows
):
    order = order_ref[...]
    square = order * order
    cosine = [jnp.broadcast_to(cos_ref[:, h * 128 : h * 128 + 128], (CP, 128)) for h in range(2)]
    diag = [diag_ref[:, h * 128 : h * 128 + 128] for h in range(2)]
    zero = order * 0.0

    def step(degree, state):
        deg = jnp.full((CP, 128), degree, jnp.int32).astype(F32)
        back = deg - 1.0
        up = jnp.sqrt(jnp.maximum(4.0 * deg * deg - 1.0, 0.0) / jnp.maximum(deg * deg - square, 1.0))
        down = jnp.sqrt(
            jnp.maximum(back * back - square, 0.0) / jnp.maximum(4.0 * back * back - 1.0, 1.0)
        )
        new = []
        for h in range(2):
            previous, earlier = state[2 * h], state[2 * h + 1]
            entry = (up * cosine[h]) * previous - (up * down) * earlier
            entry = jnp.where(order == deg, diag[h], entry)
            rows[h, pl.ds(pl.multiple_of(degree * CP, CP), CP), :] = entry
            new += [entry, previous]
        return tuple(new)

    lax.fori_loop(0, M, step, (zero,) * 4, unroll=8)
    for m in range(ML):
        for h in range(2):
            out_ref[m, :, h * 128 : h * 128 + 128] = rows.at[h][
                pl.ds(m, M, stride=CP), :
            ].astype(BF)


def forward_kernel(
    recv_ref, u_ref, v_ref, c_ref, s_ref, out_ref, grid, rows, stage, out_sems
):
    pieces = [
        jnp.concatenate([recv_ref[hi * 8 + lo].astype(F32) for hi in range(4)], axis=0)
        for lo in range(8)
    ]
    pieces = swap_blocks(pieces, 16)
    for hi in range(4):
        for lo in range(8):
            grid.at[hi][pl.ds(lo, 24, stride=8), :] = pieces[lo][hi * 24 : hi * 24 + 24]
        grid[hi, 192:256, :] = jnp.zeros((64, 128), F32)
    circles = jnp.concatenate([grid[hi].astype(BF) for hi in range(4)], axis=1)
    cosb, sinb = c_ref[...], s_ref[...]
    table = jnp.concatenate(
        [
            (u_ref[s : s + 1, :] * cosb + v_ref[s : s + 1, :] * sinb).astype(BF)
            for s in range(PLON)
        ],
        axis=0,
    )
    spectra = jnp.dot(circles, table, preferred_element_type=F32)
    copies = []
    for b in range(3):
        turned = spectra[:, 128 * b : 128 * b + 128].T
        for g in range(2):
            rows[pl.ds(256 * b + g, 128, stride=2), :] = turned[:, g * 128 : g * 128 + 128]
        first, last = ((0, 5), (5, 10), (10, PLAT))[b]
        for e in range(first, last):
            stage[e] = rows[48 * e : 48 * e + 48, :].astype(BF)
        copies.append(send(stage, out_ref, out_sems, b, first, last - first))
    for copy in copies:
        copy.wait()


def split(value):
    high = value.astype(BF)
    low = (value - high.astype(F32)).astype(BF)
    return jnp.concatenate([high, low], axis=0)


def legendre_kernel(
    recv_ref, tab_ref, quad_ref, gain_ref, out_ref, grid, res, stage, out_sems
):
    pieces = [
        jnp.concatenate([recv_ref[hi * 8 + lo].astype(F32) for hi in range(2)], axis=0)
        for lo in range(8)
    ]
    pieces = swap_blocks(pieces, 16)
    for hi in range(2):
        for x in range(8):
            grid.at[hi][pl.ds(x, 48, stride=8), :] = pieces[x][hi * 48 : hi * 48 + 48]
    gain = gain_ref[...]
    quad = quad_ref[...]
    for m in range(ML):
        part = slice(32 * m, 32 * m + 32)
        weighted = jnp.concatenate([grid[0, part, :], grid[1, part, :]], axis=1) * quad
        table = tab_ref[m]
        both = lax.dot_general(split(weighted), table, NT, preferred_element_type=F32)
        harmonics = (both[:32] + both[32:]) * gain
        both = jnp.dot(split(harmonics), table, preferred_element_type=F32)
        result = both[:32] + both[32:]
        for r in range(2):
            at = (2 * m + r) * CL
            for h in range(2):
                res[h, at : at + CL, :] = result[16 * r : 16 * r + CL, h * 128 : h * 128 + 128]
    lanes = lax.broadcasted_iota(jnp.int32, (48, 128), 1)
    source = [[res.at[h][pl.ds(lo, 48, stride=6), :] for lo in range(6)] for h in range(2)]
    copies = []
    for j in range(PLAT):
        total = None
        for lo in range(6):
            shift = (lo * AX - (16 * j - RLAT)) % 128
            value = pltpu.roll(source[j // 8][lo], shift, 1) if shift else source[j // 8][lo]
            if j in (7, 8):
                other = source[1 - j // 8][lo]
                other = pltpu.roll(other, shift, 1) if shift else other
                bound = 128 - (16 * 7 - RLAT) if j == 7 else RLAT
                first, last = (value, other) if j == 7 else (other, value)
                value = jnp.where(lanes < lo * AX + bound, first, last)
            total = value if total is None else jnp.where(lanes >= lo * AX, value, total)
        stage[j] = total.astype(BF)
        if j % 4 == 3:
            copies.append(send(stage, out_ref, out_sems, j // 4, j - 3, 4))
    for copy in copies:
        copy.wait()


def inverse_kernel(
    recv_ref, u_ref, v_ref, c_ref, s_ref, out_ref, rows, coef, grid, stage, out_sems
):
    for e in range(PLAT):
        rows[48 * e : 48 * e + 48, :] = recv_ref[e].astype(F32)
    for hi in range(2):
        turned = rows[pl.ds(hi, 2 * M, stride=2), :].T
        coef[hi * 6 * AX : (hi + 1) * 6 * AX, :] = turned[: 6 * AX, :]
    left = coef[...].astype(BF)
    cosb, sinb = c_ref[...], s_ref[...]
    copies = []
    for k in range(8):
        table = jnp.concatenate(
            [
                (u_ref[d : d + 1, :] * cosb + v_ref[d : d + 1, :] * sinb).astype(BF)
                for d in range(4 * k, 4 * k + 4)
            ],
            axis=0,
        )
        grid[k] = lax.dot_general(left, table, NT, preferred_element_type=F32)
        pieces = [grid.at[k][pl.ds(lo, 60, stride=4), :] for lo in range(4)]
        pieces = swap_blocks(pieces, 32)
        for lo in range(4):
            stage[4 * k + lo] = pieces[lo].astype(BF)
        copies.append(send(stage, out_ref, out_sems, k, 4 * k, 4))
    for copy in copies:
        copy.wait()


def gather_rows(taps_ref, field, mixing_ref, gathered, rows, cols, wide, start):
    for a in range(rows):
        bands = []
        for k in range(KB):
            line = taps_ref[k, a : a + 1, :]
            band = pltpu.roll(
                jnp.broadcast_to(line, (cols, LANES)), start, 1, stride=1, stride_axis=0
            )
            bands.append(band.astype(BF))
        band = jnp.concatenate(bands, axis=0)[:, : DLAT * wide]
        value = jnp.dot(
            band, field[a * wide : (a + DLAT) * wide, :], preferred_element_type=F32
        ).astype(BF)
        for k in range(KB):
            gathered[k, a * cols : (a + 1) * cols, :] = value[k * cols : (k + 1) * cols]
    total = jnp.dot(gathered[0], mixing_ref[0], preferred_element_type=F32)
    for k in range(1, KB):
        total += jnp.dot(gathered[k], mixing_ref[k], preferred_element_type=F32)
    return total


def edge_kernel(fields_ref, stencil_ref, reach_ref, up_ref, down_ref, taps_ref):
    place_taps(stencil_ref, reach_ref, taps_ref, 48)
    for out_ref, first, line in ((up_ref, A - EDGE, A - RLAT), (down_ref, 0, 0)):
        for a in range(EDGE):
            out_ref[N * a : N * a + N, :] = fields_ref[first + a]
        lines = [taps_ref[k, line : line + RLAT, :] for k in range(KB)]
        lines = jnp.concatenate(lines + [jnp.zeros((N - KB * RLAT, LANES), F32)], axis=0)
        lines = jnp.concatenate([lines, jnp.zeros((N, C - LANES), F32)], axis=1)
        out_ref[N * EDGE : N * EDGE + N, :] = lines.astype(BF)


def rim_row(a, fields_ref, above_ref, below_ref):
    if a < EDGE:
        return above_ref[N * a : N * a + N, :]
    if a < A + EDGE:
        return fields_ref[a - EDGE]
    return below_ref[N * (a - A - EDGE) : N * (a - A - EDGE) + N, :]


def rim_kernel(fields_ref, above_ref, below_ref, left_ref, right_ref, ahead, behind):
    for a in range(AX + EDGE):
        row = rim_row(a, fields_ref, above_ref, below_ref).astype(F32)
        ahead[HALO * a : HALO * a + HALO, :] = row[N - HALO :]
        behind[HALO * a : HALO * a + HALO, :] = row[:HALO]
    right_ref[...] = ahead[...].astype(BF)
    left_ref[...] = behind[...].astype(BF)


def first_kernel(
    fields_ref, left_ref, right_ref, above_ref, below_ref, taps_ref, mix_ref, out_ref,
    field, taps, gathered, before, after,
):
    before[...] = left_ref[...].astype(F32)
    after[...] = right_ref[...].astype(F32)
    gap = jnp.zeros((N - HALO, C), F32)
    for a in range(AX + EDGE):
        part = slice(HALO * a, HALO * a + HALO)
        own = rim_row(a, fields_ref, above_ref, below_ref).astype(F32)
        row = jnp.concatenate([gap, before[part, :], own, after[part, :], gap], axis=0)
        field[48 * a : 48 * a + 48, :] = row.astype(BF)
    top = above_ref[N * EDGE : N * EDGE + N, :].astype(F32)
    bottom = below_ref[N * EDGE : N * EDGE + N, :].astype(F32)
    for k in range(KB):
        part = slice(RLAT * k, RLAT * k + RLAT)
        taps[k, :RLAT, :] = top[part, :LANES]
        taps[k, RLAT : RLAT + A, :] = taps_ref[k]
        taps[k, RLAT + A : AX, :] = bottom[part, :LANES]
    first = gather_rows(taps, field, mix_ref, gathered, AX, JX, 48, 16 - OFF - RLON)
    for a in range(AX):
        own = field[(a + RLAT) * 48 : (a + RLAT) * 48 + 48, :].astype(F32)
        value = first[a * JX : (a + 1) * JX] + own[16 - OFF : 16 - OFF + JX]
        out_ref[a * JX : (a + 1) * JX, :] = value.astype(BF)


def lines_kernel(stencil_ref, reach_ref, taps_ref):
    place_taps(stencil_ref, reach_ref, taps_ref, JX)


def last_kernel(
    place_ref, recv_ref, pre_ref, taps_ref, norm_ref, mix_ref, in_ref, back_ref, out_ref,
    rows, stream, exact, gathered,
):
    place = place_ref[0]
    for s in range(PLON):
        rows[60 * s : 60 * s + 60, :] = recv_ref[s].astype(F32)
    for hi in range(5):
        spectral = rows[pl.ds(hi, C, stride=5), :].T
        value = pre_ref[128 * hi : 128 * hi + 128, :].astype(F32) + spectral
        row = lax.broadcasted_iota(jnp.int32, (128, C), 0) // JX + 4 * hi - RLAT + place * A
        value = jnp.where((row >= 0) & (row < NLAT), value, 0.0).astype(BF)
        stream[128 * hi : 128 * hi + 128, :] = value
        exact[128 * hi : 128 * hi + 128, :] = value.astype(F32)
    second = gather_rows(taps_ref, stream, mix_ref, gathered, A, N, JX, OFF - RLON)
    own = jnp.concatenate(
        [exact[(a + RLAT) * JX + OFF : (a + RLAT) * JX + OFF + N, :] for a in range(A)], axis=0
    )
    summed = own + second
    center = summed - jnp.mean(summed, axis=-1, keepdims=True)
    spread = jnp.mean(center * center, axis=-1, keepdims=True)
    normed = (center * lax.rsqrt(spread + 1e-05) * norm_ref[...]).astype(BF)
    hidden = jax.nn.gelu(jnp.dot(normed, in_ref[...], preferred_element_type=F32)).astype(BF)
    update = jnp.dot(hidden, back_ref[...], preferred_element_type=F32)
    out_ref[...] = (own + update).astype(BF).reshape(A, N, C)


def legendre_start(colatitude, orders, degrees):
    order_vals = orders.astype(F32)
    counter = jnp.arange(1, degrees + 1, dtype=jnp.int32).astype(F32)
    factors = jnp.log((2.0 * counter - 1.0) / (2.0 * counter))
    partial_sum = jnp.sum(
        jnp.where(counter[None, :] <= order_vals[:, None], factors[None, :], 0.0), axis=1
    )
    log_sine = jnp.log(jnp.sin(colatitude))
    start_log = 0.5 * jnp.log((2.0 * order_vals + 1.0) / (4.0 * math.pi)) + 0.5 * partial_sum
    return jnp.exp(start_log[:, None] + order_vals[:, None] * log_sine[None, :])


def shifted(value, axis, by, closed):
    count = lax.axis_size(axis)
    pairs = [(i, (i + by) % count) for i in range(count) if closed or 0 <= i + by < count]
    return lax.ppermute(value, axis, pairs)


def exchange(block, axis):
    return lax.all_to_all(block, axis, split_axis=0, concat_axis=0, tiled=True)


def shape(dims, dtype):
    return jax.ShapeDtypeStruct(dims, dtype)


def local(
    fields, spectral_gain, stencil_one, stencil_two, cycle_reach, mix_one, mix_two, norm_gain,
    w_in, w_out,
):
    place = lax.axis_index("lat")
    colatitude = math.pi * (jnp.arange(NLAT, dtype=jnp.int32).astype(F32) + 0.5) / NLAT
    quad = math.pi / NLAT * (2.0 * math.pi / NLON) * jnp.sin(colatitude)
    own_orders = place * ML + jnp.minimum(jnp.arange(CP, dtype=jnp.int32), ML - 1)
    diagonal = legendre_start(colatitude, own_orders, M)

    sent = call(
        prep_kernel,
        shape((PLON, 24, 128), BF),
        [
            pltpu.VMEM((3, A, N, 128), BF),
            pltpu.VMEM((768, 128), F32),
            pltpu.SemaphoreType.DMA((3,)),
            pltpu.VMEM((PLON, 24, 128), BF),
            pltpu.SemaphoreType.DMA((3,)),
        ],
        fields,
        out=pl.ANY,
        hbm=(0,),
        limit=LAST_LIMIT,
        moved=1.1,
    )
    sent, late_place, late_orders = lax.optimization_barrier(
        (sent, place.reshape(1), own_orders)
    )
    recv = exchange(sent, "lon")
    factors = call(
        twiddle_kernel,
        [
            shape((rows, 2 * M), F32)
            for rows in (PLON, PLON, N, N, PLON, PLON, JX, JX)
        ],
        [],
        late_place,
        smem=(0,),
        moved=0.4,
    )

    def by_offset(stencil):
        return jnp.transpose(stencil, (1, 2, 0, 3)).reshape(KB * DLAT, A, TAPS)

    table = call(
        table_kernel,
        shape((ML, M, NLAT), BF),
        [pltpu.VMEM((2, M * CP, 128), F32)],
        jnp.broadcast_to(late_orders.astype(F32)[:, None], (CP, 128)),
        jnp.cos(colatitude)[None, :],
        diagonal,
        moved=3.3,
    )
    recv, table = lax.optimization_barrier((recv, table))
    spectra = call(
        forward_kernel,
        shape((PLAT, 48, 128), BF),
        [
            pltpu.VMEM((4, 256, 128), F32),
            pltpu.VMEM((768, 128), F32),
            pltpu.VMEM((PLAT, 48, 128), BF),
            pltpu.SemaphoreType.DMA((3,)),
        ],
        recv,
        *factors[:4],
        out=pl.ANY,
        moved=1.4,
    )
    up, down, taps_one = call(
        edge_kernel,
        [shape((N * EDGE + N, C), BF)] * 2 + [shape((KB, A, LANES), F32)],
        [],
        fields,
        by_offset(stencil_one),
        cycle_reach,
        smem=(2,),
        moved=0.7,
    )
    spectra, up, down = lax.optimization_barrier((spectra, up, down))
    gathered = exchange(spectra, "lat")
    above = shifted(up, "lat", 1, False)
    below = shifted(down, "lat", -1, False)
    gain = jnp.pad(spectral_gain.T, ((0, CP - CL), (0, 0)))
    results = call(
        legendre_kernel,
        shape((PLAT, 48, 128), BF),
        [
            pltpu.VMEM((2, 384, 128), F32),
            pltpu.VMEM((2, 288, 128), F32),
            pltpu.VMEM((PLAT, 48, 128), BF),
            pltpu.SemaphoreType.DMA((4,)),
        ],
        gathered,
        table,
        quad[None, :],
        jnp.concatenate([gain, gain], axis=0),
        out=pl.ANY,
        moved=2.6,
    )
    results, above, below = lax.optimization_barrier((results, above, below))
    returned = exchange(results, "lat")
    to_left, to_right = call(
        rim_kernel,
        [shape((HALO * (AX + EDGE), C), BF)] * 2,
        [pltpu.VMEM((HALO * (AX + EDGE), C), F32)] * 2,
        fields,
        above,
        below,
        moved=0.5,
    )
    left = shifted(to_right, "lon", 1, True)
    right = shifted(to_left, "lon", -1, True)
    sectors = call(
        inverse_kernel,
        shape((PLON, 60, 128), BF),
        [
            pltpu.VMEM((768, 128), F32),
            pltpu.VMEM((CL * AX, 2 * M), F32),
            pltpu.VMEM((8, CL * AX, 128), F32),
            pltpu.VMEM((PLON, 60, 128), BF),
            pltpu.SemaphoreType.DMA((8,)),
        ],
        returned,
        *factors[4:],
        out=pl.ANY,
        moved=1.7,
    )
    spectral = exchange(sectors, "lon")
    pre = call(
        first_kernel,
        shape((AX * JX, C), BF),
        [
            pltpu.VMEM(((AX + EDGE) * 48, C), BF),
            pltpu.VMEM((KB, 24, LANES), F32),
            pltpu.VMEM((KB, AX * JX, C), BF),
            pltpu.VMEM((HALO * (AX + EDGE), C), F32),
            pltpu.VMEM((HALO * (AX + EDGE), C), F32),
        ],
        fields,
        left,
        right,
        above,
        below,
        taps_one,
        mix_one,
        moved=0.1,
    )
    pre, late_two = lax.optimization_barrier((pre, by_offset(stencil_two)))
    taps_two = call(
        lines_kernel,
        shape((KB, A, LANES), F32),
        [],
        late_two,
        cycle_reach,
        smem=(1,),
        moved=20.0,
    )
    return call(
        last_kernel,
        shape((A, N, C), BF),
        [
            pltpu.VMEM((1920, 128), F32),
            pltpu.VMEM((AX * JX, C), BF),
            pltpu.VMEM((AX * JX, C), F32),
            pltpu.VMEM((KB, A * N, C), BF),
        ],
        place.reshape(1),
        spectral,
        pre,
        taps_two,
        norm_gain[None, :],
        mix_two,
        w_in,
        w_out,
        smem=(0,),
        moved=2.7,
    )


def solution(mesh):
    in_specs = (
        P("lat", "lon", None),
        P(None, "lon"),
        P("lat", None, None, None),
        P("lat", None, None, None),
        P("lat"),
        P(),
        P(),
        P(),
        P(),
        P(),
    )
    out_specs = P("lat", "lon", None)
    return jax.shard_map(local, mesh=mesh, in_specs=in_specs, out_specs=out_specs, check_vma=False)
```

```python
import functools
import math

import jax
import jax.numpy as jnp
from jax import lax
from jax.experimental import pallas as pl
from jax.experimental.pallas import tpu as pltpu
from jax.sharding import PartitionSpec as P

C = 384
CL = 12
CP = 16
KB = 3
RLAT = 2
RLON = 6
TAPS = 2 * RLON + 1
DLAT = 2 * RLAT + 1
NLAT = 256
NLON = 512
PLAT = 16
PLON = 32
A = 16
N = 16
M = 192
ML = 12
AX = A + 2 * RLAT
JX = 32
OFF = 8
LANES = 256
EDGE = 2 * RLAT
HALO = 2 * RLON
F32 = jnp.float32
BF = jnp.bfloat16
NT = (((1,), (1,)), ((), ()))
VMEM_LIMIT = 14 * 1024 * 1024
LAST_LIMIT = 61 * 1024 * 1024


def call(kernel, outs, scratch, *args, smem=(), hbm=(), limit=VMEM_LIMIT, moved=1.0):
    specs = [
        pl.BlockSpec(
            memory_space=pltpu.SMEM if i in smem else pltpu.HBM if i in hbm else pltpu.VMEM
        )
        for i in range(len(args))
    ]
    out_specs = jax.tree.map(lambda _: pl.BlockSpec(memory_space=pltpu.VMEM), outs)
    return pl.pallas_call(
        kernel,
        out_shape=outs,
        in_specs=specs,
        out_specs=out_specs,
        scratch_shapes=scratch,
        cost_estimate=pl.CostEstimate(
            flops=int(moved * 500_000_000), bytes_accessed=int(moved * 3_400_000), transcendentals=0
        ),
        compiler_params=pltpu.CompilerParams(vmem_limit_bytes=limit),
    )(*args)


def swap_blocks(pieces, width):
    count = len(pieces)
    pieces = list(pieces)
    block = lax.broadcasted_iota(jnp.int32, pieces[0].shape, 1) // width
    step = 1
    while step < count:
        low = (block & step) == 0
        for i in range(count):
            if i & step:
                continue
            x, y = pieces[i], pieces[i | step]
            pieces[i] = jnp.where(low, x, pltpu.roll(y, step * width, 1))
            pieces[i | step] = jnp.where(low, pltpu.roll(x, 128 - step * width, 1), y)
        step *= 2
    return pieces


def prep_kernel(fields_ref, out_ref, field, rows, sems):
    copies = [
        pltpu.make_async_copy(
            fields_ref.at[:, :, pl.ds(128 * g, 128)], field.at[g], sems.at[g]
        )
        for g in range(3)
    ]
    for copy in copies:
        copy.start()
    for g in range(3):
        copies[g].wait()
        turned = field[g].reshape(A * N, 128).astype(F32).T
        for hi in range(2):
            rows[pl.ds(256 * g + hi, 128, stride=2), :] = turned[:, hi * 128 : hi * 128 + 128]
    for d in range(PLON):
        out_ref[d] = rows[24 * d : 24 * d + 24, :].astype(BF)


def twiddle_kernel(place_ref, u_ref, v_ref, c_ref, s_ref, iu_ref, iv_ref, ic_ref, is_ref):
    lane = lax.broadcasted_iota(jnp.int32, (PLON, 2 * M), 1)
    row = lax.broadcasted_iota(jnp.int32, (PLON, 2 * M), 0)
    order = lane // 2

    def turn(product):
        return 2.0 * math.pi / NLON * (product & (NLON - 1)).astype(F32)

    outer = turn(row * N * order + (lane & 1) * (NLON // 4))
    cos, sin = jnp.cos(outer), -jnp.sin(outer)
    scale = jnp.where(order == 0, 1.0, 2.0)
    u_ref[...], v_ref[...] = cos, sin
    iu_ref[...], iv_ref[...] = cos * scale, sin * scale
    inner = turn((row - OFF) * order)
    cos, sin = jnp.cos(inner), jnp.sin(inner)
    ic_ref[...], is_ref[...] = cos, sin
    c_ref[...], s_ref[...] = cos[OFF : OFF + N], sin[OFF : OFF + N]


def place_taps(stencil_ref, reach_ref, out_ref, wide):
    offset = lax.broadcasted_iota(jnp.int32, (A, TAPS), 1) - RLON
    cycle = lax.broadcasted_iota(jnp.int32, (A, TAPS), 0)
    reach = jnp.zeros((A, TAPS), jnp.int32)
    for a in range(A):
        reach = jnp.where(cycle == a, reach_ref[a], reach)
    inside = jnp.abs(offset) <= reach
    for k in range(KB):
        total = None
        for d in range(DLAT):
            taps = jnp.where(inside, stencil_ref[k * DLAT + d].astype(F32), 0.0)
            taps = jnp.concatenate([taps, jnp.zeros((A, LANES - TAPS), F32)], axis=1)
            taps = pltpu.roll(taps, d * wide, 1) if d else taps
            total = taps if total is None else total + taps
        out_ref[k] = total


def table_kernel(
    order_ref, cos_ref, diag_ref, out_ref, rows
):
    order = order_ref[...]
    square = order * order
    cosine = [jnp.broadcast_to(cos_ref[:, h * 128 : h * 128 + 128], (CP, 128)) for h in range(2)]
    diag = [diag_ref[:, h * 128 : h * 128 + 128] for h in range(2)]
    zero = order * 0.0

    def step(degree, state):
        deg = jnp.full((CP, 128), degree, jnp.int32).astype(F32)
        back = deg - 1.0
        up = jnp.sqrt(jnp.maximum(4.0 * deg * deg - 1.0, 0.0) / jnp.maximum(deg * deg - square, 1.0))
        down = jnp.sqrt(
            jnp.maximum(back * back - square, 0.0) / jnp.maximum(4.0 * back * back - 1.0, 1.0)
        )
        new = []
        for h in range(2):
            previous, earlier = state[2 * h], state[2 * h + 1]
            entry = (up * cosine[h]) * previous - (up * down) * earlier
            entry = jnp.where(order == deg, diag[h], entry)
            rows[h, pl.ds(pl.multiple_of(degree * CP, CP), CP), :] = entry
            new += [entry, previous]
        return tuple(new)

    lax.fori_loop(0, M, step, (zero,) * 4, unroll=8)
    for m in range(ML):
        for h in range(2):
            out_ref[m, :, h * 128 : h * 128 + 128] = rows.at[h][
                pl.ds(m, M, stride=CP), :
            ].astype(BF)


def forward_kernel(recv_ref, u_ref, v_ref, c_ref, s_ref, out_ref, grid, rows):
    pieces = [
        jnp.concatenate([recv_ref[hi * 8 + lo].astype(F32) for hi in range(4)], axis=0)
        for lo in range(8)
    ]
    pieces = swap_blocks(pieces, 16)
    for hi in range(4):
        for lo in range(8):
            grid.at[hi][pl.ds(lo, 24, stride=8), :] = pieces[lo][hi * 24 : hi * 24 + 24]
        grid[hi, 192:256, :] = jnp.zeros((64, 128), F32)
    circles = jnp.concatenate([grid[hi].astype(BF) for hi in range(4)], axis=1)
    cosb, sinb = c_ref[...], s_ref[...]
    table = jnp.concatenate(
        [
            (u_ref[s : s + 1, :] * cosb + v_ref[s : s + 1, :] * sinb).astype(BF)
            for s in range(PLON)
        ],
        axis=0,
    )
    spectra = jnp.dot(circles, table, preferred_element_type=F32).T
    for g in range(2):
        rows[pl.ds(g, 2 * M, stride=2), :] = spectra[:, g * 128 : g * 128 + 128]
    for e in range(PLAT):
        out_ref[e] = rows[48 * e : 48 * e + 48, :].astype(BF)


def split(value):
    high = value.astype(BF)
    low = (value - high.astype(F32)).astype(BF)
    return jnp.concatenate([high, low], axis=0)


def legendre_kernel(recv_ref, tab_ref, quad_ref, gain_ref, out_ref, grid, res):
    pieces = [
        jnp.concatenate([recv_ref[hi * 8 + lo].astype(F32) for hi in range(2)], axis=0)
        for lo in range(8)
    ]
    pieces = swap_blocks(pieces, 16)
    for hi in range(2):
        for x in range(8):
            grid.at[hi][pl.ds(x, 48, stride=8), :] = pieces[x][hi * 48 : hi * 48 + 48]
    gain = gain_ref[...]
    quad = quad_ref[...]
    for m in range(ML):
        part = slice(32 * m, 32 * m + 32)
        weighted = jnp.concatenate([grid[0, part, :], grid[1, part, :]], axis=1) * quad
        table = tab_ref[m]
        both = lax.dot_general(split(weighted), table, NT, preferred_element_type=F32)
        harmonics = (both[:32] + both[32:]) * gain
        both = jnp.dot(split(harmonics), table, preferred_element_type=F32)
        result = both[:32] + both[32:]
        for r in range(2):
            at = (2 * m + r) * CL
            for h in range(2):
                res[h, at : at + CL, :] = result[16 * r : 16 * r + CL, h * 128 : h * 128 + 128]
    lanes = lax.broadcasted_iota(jnp.int32, (48, 128), 1)
    source = [[res.at[h][pl.ds(lo, 48, stride=6), :] for lo in range(6)] for h in range(2)]
    for j in range(PLAT):
        total = None
        for lo in range(6):
            shift = (lo * AX - (16 * j - RLAT)) % 128
            value = pltpu.roll(source[j // 8][lo], shift, 1) if shift else source[j // 8][lo]
            if j in (7, 8):
                other = source[1 - j // 8][lo]
                other = pltpu.roll(other, shift, 1) if shift else other
                bound = 128 - (16 * 7 - RLAT) if j == 7 else RLAT
                first, last = (value, other) if j == 7 else (other, value)
                value = jnp.where(lanes < lo * AX + bound, first, last)
            total = value if total is None else jnp.where(lanes >= lo * AX, value, total)
        out_ref[j] = total.astype(BF)


def inverse_kernel(recv_ref, u_ref, v_ref, c_ref, s_ref, out_ref, rows, coef, grid):
    for e in range(PLAT):
        rows[48 * e : 48 * e + 48, :] = recv_ref[e].astype(F32)
    for hi in range(2):
        turned = rows[pl.ds(hi, 2 * M, stride=2), :].T
        coef[hi * 6 * AX : (hi + 1) * 6 * AX, :] = turned[: 6 * AX, :]
    left = coef[...].astype(BF)
    cosb, sinb = c_ref[...], s_ref[...]
    for k in range(8):
        table = jnp.concatenate(
            [
                (u_ref[d : d + 1, :] * cosb + v_ref[d : d + 1, :] * sinb).astype(BF)
                for d in range(4 * k, 4 * k + 4)
            ],
            axis=0,
        )
        grid[k] = lax.dot_general(left, table, NT, preferred_element_type=F32)
    for k in range(8):
        pieces = [grid.at[k][pl.ds(lo, 60, stride=4), :] for lo in range(4)]
        pieces = swap_blocks(pieces, 32)
        for lo in range(4):
            out_ref[4 * k + lo] = pieces[lo].astype(BF)


def gather_rows(taps_ref, field, mixing_ref, gathered, rows, cols, wide, start):
    for a in range(rows):
        bands = []
        for k in range(KB):
            line = taps_ref[k, a : a + 1, :]
            band = pltpu.roll(
                jnp.broadcast_to(line, (cols, LANES)), start, 1, stride=1, stride_axis=0
            )
            bands.append(band.astype(BF))
        band = jnp.concatenate(bands, axis=0)[:, : DLAT * wide]
        value = jnp.dot(
            band, field[a * wide : (a + DLAT) * wide, :], preferred_element_type=F32
        ).astype(BF)
        for k in range(KB):
            gathered[k, a * cols : (a + 1) * cols, :] = value[k * cols : (k + 1) * cols]
    total = jnp.dot(gathered[0], mixing_ref[0], preferred_element_type=F32)
    for k in range(1, KB):
        total += jnp.dot(gathered[k], mixing_ref[k], preferred_element_type=F32)
    return total


def edge_kernel(fields_ref, stencil_ref, reach_ref, up_ref, down_ref, taps_ref):
    place_taps(stencil_ref, reach_ref, taps_ref, 48)
    for out_ref, first, line in ((up_ref, A - EDGE, A - RLAT), (down_ref, 0, 0)):
        for a in range(EDGE):
            out_ref[N * a : N * a + N, :] = fields_ref[first + a]
        lines = [taps_ref[k, line : line + RLAT, :] for k in range(KB)]
        lines = jnp.concatenate(lines + [jnp.zeros((N - KB * RLAT, LANES), F32)], axis=0)
        lines = jnp.concatenate([lines, jnp.zeros((N, C - LANES), F32)], axis=1)
        out_ref[N * EDGE : N * EDGE + N, :] = lines.astype(BF)


def rim_row(a, fields_ref, above_ref, below_ref):
    if a < EDGE:
        return above_ref[N * a : N * a + N, :]
    if a < A + EDGE:
        return fields_ref[a - EDGE]
    return below_ref[N * (a - A - EDGE) : N * (a - A - EDGE) + N, :]


def rim_kernel(fields_ref, above_ref, below_ref, left_ref, right_ref, ahead, behind):
    for a in range(AX + EDGE):
        row = rim_row(a, fields_ref, above_ref, below_ref).astype(F32)
        ahead[HALO * a : HALO * a + HALO, :] = row[N - HALO :]
        behind[HALO * a : HALO * a + HALO, :] = row[:HALO]
    right_ref[...] = ahead[...].astype(BF)
    left_ref[...] = behind[...].astype(BF)


def first_kernel(
    fields_ref, left_ref, right_ref, above_ref, below_ref, taps_ref, mix_ref, out_ref,
    field, taps, gathered, before, after,
):
    before[...] = left_ref[...].astype(F32)
    after[...] = right_ref[...].astype(F32)
    gap = jnp.zeros((N - HALO, C), F32)
    for a in range(AX + EDGE):
        part = slice(HALO * a, HALO * a + HALO)
        own = rim_row(a, fields_ref, above_ref, below_ref).astype(F32)
        row = jnp.concatenate([gap, before[part, :], own, after[part, :], gap], axis=0)
        field[48 * a : 48 * a + 48, :] = row.astype(BF)
    top = above_ref[N * EDGE : N * EDGE + N, :].astype(F32)
    bottom = below_ref[N * EDGE : N * EDGE + N, :].astype(F32)
    for k in range(KB):
        part = slice(RLAT * k, RLAT * k + RLAT)
        taps[k, :RLAT, :] = top[part, :LANES]
        taps[k, RLAT : RLAT + A, :] = taps_ref[k]
        taps[k, RLAT + A : AX, :] = bottom[part, :LANES]
    first = gather_rows(taps, field, mix_ref, gathered, AX, JX, 48, 16 - OFF - RLON)
    for a in range(AX):
        own = field[(a + RLAT) * 48 : (a + RLAT) * 48 + 48, :].astype(F32)
        value = first[a * JX : (a + 1) * JX] + own[16 - OFF : 16 - OFF + JX]
        out_ref[a * JX : (a + 1) * JX, :] = value.astype(BF)


def lines_kernel(stencil_ref, reach_ref, taps_ref):
    place_taps(stencil_ref, reach_ref, taps_ref, JX)


def last_kernel(
    place_ref, recv_ref, pre_ref, taps_ref, norm_ref, mix_ref, in_ref, back_ref, out_ref,
    rows, stream, gathered,
):
    place = place_ref[0]
    for s in range(PLON):
        rows[60 * s : 60 * s + 60, :] = recv_ref[s].astype(F32)
    for hi in range(5):
        spectral = rows[pl.ds(hi, C, stride=5), :].T
        value = pre_ref[128 * hi : 128 * hi + 128, :].astype(F32) + spectral
        row = lax.broadcasted_iota(jnp.int32, (128, C), 0) // JX + 4 * hi - RLAT + place * A
        value = jnp.where((row >= 0) & (row < NLAT), value, 0.0).astype(BF)
        stream[128 * hi : 128 * hi + 128, :] = value
    second = gather_rows(taps_ref, stream, mix_ref, gathered, A, N, JX, OFF - RLON)
    own = jnp.concatenate(
        [
            stream[(a + RLAT) * JX : (a + RLAT + 1) * JX, :].astype(F32)[OFF : OFF + N]
            for a in range(A)
        ],
        axis=0,
    )
    summed = own + second
    center = summed - jnp.mean(summed, axis=-1, keepdims=True)
    spread = jnp.mean(center * center, axis=-1, keepdims=True)
    normed = (center * lax.rsqrt(spread + 1e-05) * norm_ref[...]).astype(BF)
    hidden = jax.nn.gelu(jnp.dot(normed, in_ref[...], preferred_element_type=F32)).astype(BF)
    update = jnp.dot(hidden, back_ref[...], preferred_element_type=F32)
    out_ref[...] = (own + update).astype(BF).reshape(A, N, C)


def legendre_start(colatitude, orders, degrees):
    order_vals = orders.astype(F32)
    counter = jnp.arange(1, degrees + 1, dtype=jnp.int32).astype(F32)
    factors = jnp.log((2.0 * counter - 1.0) / (2.0 * counter))
    partial_sum = jnp.sum(
        jnp.where(counter[None, :] <= order_vals[:, None], factors[None, :], 0.0), axis=1
    )
    log_sine = jnp.log(jnp.sin(colatitude))
    start_log = 0.5 * jnp.log((2.0 * order_vals + 1.0) / (4.0 * math.pi)) + 0.5 * partial_sum
    return jnp.exp(start_log[:, None] + order_vals[:, None] * log_sine[None, :])


def shifted(value, axis, by, closed):
    count = lax.axis_size(axis)
    pairs = [(i, (i + by) % count) for i in range(count) if closed or 0 <= i + by < count]
    return lax.ppermute(value, axis, pairs)


def exchange(block, axis):
    return lax.all_to_all(block, axis, split_axis=0, concat_axis=0, tiled=True)


def shape(dims, dtype):
    return jax.ShapeDtypeStruct(dims, dtype)


def local(
    fields, spectral_gain, stencil_one, stencil_two, cycle_reach, mix_one, mix_two, norm_gain,
    w_in, w_out,
):
    place = lax.axis_index("lat")
    colatitude = math.pi * (jnp.arange(NLAT, dtype=jnp.int32).astype(F32) + 0.5) / NLAT
    quad = math.pi / NLAT * (2.0 * math.pi / NLON) * jnp.sin(colatitude)
    own_orders = place * ML + jnp.minimum(jnp.arange(CP, dtype=jnp.int32), ML - 1)
    diagonal = legendre_start(colatitude, own_orders, M)

    sent = call(
        prep_kernel,
        shape((PLON, 24, 128), BF),
        [
            pltpu.VMEM((3, A, N, 128), BF),
            pltpu.VMEM((768, 128), F32),
            pltpu.SemaphoreType.DMA((3,)),
        ],
        fields,
        hbm=(0,),
        limit=LAST_LIMIT,
        moved=1.1,
    )
    sent, late_place, late_orders = lax.optimization_barrier(
        (sent, place.reshape(1), own_orders)
    )
    recv = exchange(sent, "lon")
    factors = call(
        twiddle_kernel,
        [
            shape((rows, 2 * M), F32)
            for rows in (PLON, PLON, N, N, PLON, PLON, JX, JX)
        ],
        [],
        late_place,
        smem=(0,),
        moved=0.4,
    )

    def by_offset(stencil):
        return jnp.transpose(stencil, (1, 2, 0, 3)).reshape(KB * DLAT, A, TAPS)

    table = call(
        table_kernel,
        shape((ML, M, NLAT), BF),
        [pltpu.VMEM((2, M * CP, 128), F32)],
        jnp.broadcast_to(late_orders.astype(F32)[:, None], (CP, 128)),
        jnp.cos(colatitude)[None, :],
        diagonal,
        moved=3.3,
    )
    recv, table = lax.optimization_barrier((recv, table))
    spectra = call(
        forward_kernel,
        shape((PLAT, 48, 128), BF),
        [pltpu.VMEM((4, 256, 128), F32), pltpu.VMEM((768, 128), F32)],
        recv,
        *factors[:4],
        moved=1.4,
    )
    up, down, taps_one = call(
        edge_kernel,
        [shape((N * EDGE + N, C), BF)] * 2 + [shape((KB, A, LANES), F32)],
        [],
        fields,
        by_offset(stencil_one),
        cycle_reach,
        smem=(2,),
        moved=0.7,
    )
    spectra, up, down = lax.optimization_barrier((spectra, up, down))
    gathered = exchange(spectra, "lat")
    above = shifted(up, "lat", 1, False)
    below = shifted(down, "lat", -1, False)
    gain = jnp.pad(spectral_gain.T, ((0, CP - CL), (0, 0)))
    results = call(
        legendre_kernel,
        shape((PLAT, 48, 128), BF),
        [pltpu.VMEM((2, 384, 128), F32), pltpu.VMEM((2, 288, 128), F32)],
        gathered,
        table,
        quad[None, :],
        jnp.concatenate([gain, gain], axis=0),
        moved=2.6,
    )
    results, above, below = lax.optimization_barrier((results, above, below))
    returned = exchange(results, "lat")
    to_left, to_right = call(
        rim_kernel,
        [shape((HALO * (AX + EDGE), C), BF)] * 2,
        [pltpu.VMEM((HALO * (AX + EDGE), C), F32)] * 2,
        fields,
        above,
        below,
        moved=0.5,
    )
    left = shifted(to_right, "lon", 1, True)
    right = shifted(to_left, "lon", -1, True)
    sectors = call(
        inverse_kernel,
        shape((PLON, 60, 128), BF),
        [
            pltpu.VMEM((768, 128), F32),
            pltpu.VMEM((CL * AX, 2 * M), F32),
            pltpu.VMEM((8, CL * AX, 128), F32),
        ],
        returned,
        *factors[4:],
        moved=1.7,
    )
    spectral = exchange(sectors, "lon")
    pre = call(
        first_kernel,
        shape((AX * JX, C), BF),
        [
            pltpu.VMEM(((AX + EDGE) * 48, C), BF),
            pltpu.VMEM((KB, 24, LANES), F32),
            pltpu.VMEM((KB, AX * JX, C), BF),
            pltpu.VMEM((HALO * (AX + EDGE), C), F32),
            pltpu.VMEM((HALO * (AX + EDGE), C), F32),
        ],
        fields,
        left,
        right,
        above,
        below,
        taps_one,
        mix_one,
        moved=0.1,
    )
    pre, late_two = lax.optimization_barrier((pre, by_offset(stencil_two)))
    taps_two = call(
        lines_kernel,
        shape((KB, A, LANES), F32),
        [],
        late_two,
        cycle_reach,
        smem=(1,),
        moved=20.0,
    )
    return call(
        last_kernel,
        shape((A, N, C), BF),
        [
            pltpu.VMEM((1920, 128), F32),
            pltpu.VMEM((AX * JX, C), BF),
            pltpu.VMEM((KB, A * N, C), BF),
        ],
        place.reshape(1),
        spectral,
        pre,
        taps_two,
        norm_gain[None, :],
        mix_two,
        w_in,
        w_out,
        smem=(0,),
        moved=2.7,
    )


def solution(mesh):
    in_specs = (
        P("lat", "lon", None),
        P(None, "lon"),
        P("lat", None, None, None),
        P("lat", None, None, None),
        P("lat"),
        P(),
        P(),
        P(),
        P(),
        P(),
    )
    out_specs = P("lat", "lon", None)
    return jax.shard_map(local, mesh=mesh, in_specs=in_specs, out_specs=out_specs, check_vma=False)
```
